32 devices in a mesh: grp: 2 (over x), idx: 16 (over z, y, core).
Axes of the slice: x: 2, y: 2, z: 4, core: 2. Of those that a mesh axis runs over, the one named last changes fastest.
Arguments:
- queries: bfloat16 [4096, 1024], P(('grp', 'idx')), parts along dimension 0, may hold values from -6 to 6
- rotation: float32 [1024, 1024], replicated, may hold values from -0.1875 to 0.1875
- codes: bfloat16 [1024, 128, 256], P(('grp', 'idx')), parts along dimension 0, may hold values from -0.375 to 0.375
- vectors: float32 [1024, 128, 1024], P(('grp', 'idx')), parts along dimension 0, may hold values from -0.1875 to 0.1875
- probes: int32 [128, 16], P(('grp', 'idx')), parts along dimension 0, may hold values from 0 to 511, as said below
- cand_pages: int32 [4096, 8], P(('grp', 'idx')), parts along dimension 0, may hold values from 0 to 511, as said below
- cand_rows: int32 [4096, 8], P(('grp', 'idx')), parts along dimension 0, may hold values from 0 to 127
Outputs:
- coarse: bfloat16 [4096, 2048], P(('grp', 'idx')), parts along dimension 0
- rerank: float32 [4096, 8], P(('grp', 'idx')), parts along dimension 0
The draws below stay inside these ranges and needn't reach their ends.
There are 2 independent parts, one for each index of `grp`. The reference program is written for one: setup_inputs(seed, part) draws one part's arguments, and reference() takes and returns one part's arrays. A program takes and returns all parts, laid end to end along the dimension named above; an argument that names none is the same for every part. Nothing has to cross between parts.
Inputs may be any that keep to these rules, and one draw needn't show every extreme that they name: Page j lies on index device j // 32. Among the probes of the 4 blocks of one index device, at most 8 name pages of any one index device, and the pages of one particular index device (the same one for all senders) receive exactly 8 probes from every index device. `cand_pages`: among the candidates of the 128 queries of one index device, at most 128 lie on pages of any one index device, and the pages of one particular index device (the same one for all senders) receive exactly 128 candidates from every index device.
All inputs are finite; a program needn't handle non-finite values.
Results may differ from the reference program's by a relative error of at most 0.0049.
Values may be sent and summed in bfloat16 or wider, within the bound.
No kernel may reach another device: no remote copies, remote signals or barrier semaphores. Data moves between devices by JAX's collectives and lax.ppermute only.
A program may use at most 128 MiB of HBM per device.

```python
import jax
import jax.numpy as jnp
from jax import lax

DIN = 1024
DPROJ = 256
PAGE = 128
PAGES_DEV = 32
QB = 32
NPROBE = 16
CAND = 8
SHARDS = 16
QUERIES = 2048
BLOCKS = 64
PAGES = 512
SLOTS = 64
CAP = 8
RSLOTS = 1024
RCAP = 128


def spread_owners(key, slot_count, capacity):
    key_hot, key_rows = jax.random.split(key)
    hottest = jax.random.randint(key_hot, (), 0, SHARDS)
    pool = 1 + jnp.arange((SHARDS - 1) * capacity, dtype=jnp.int32) // capacity

    def one_source(key_source):
        key_pool, key_mix = jax.random.split(key_source)
        selected_index = jax.random.permutation(key_pool, pool)[:slot_count - capacity]
        offsets = jnp.concatenate([jnp.zeros((capacity,), jnp.int32), selected_index])
        offsets = jax.random.permutation(key_mix, offsets)
        return (hottest + offsets) % SHARDS
    return jax.vmap(one_source)(jax.random.split(key_rows, SHARDS))


def draw_probes(key, part):
    key = jax.random.fold_in(key, 11)
    key_owner, key_page = jax.random.split(key)
    owners = spread_owners(key_owner, SLOTS, CAP)
    local_page = jax.random.randint(key_page, owners.shape, 0, PAGES_DEV)
    return (owners * PAGES_DEV + local_page).reshape(BLOCKS, NPROBE).astype(jnp.int32)


def draw_cand_pages(key, part):
    key = jax.random.fold_in(key, 23)
    key_owner, key_page = jax.random.split(key)
    owners = spread_owners(key_owner, RSLOTS, RCAP)
    local_page = jax.random.randint(key_page, owners.shape, 0, PAGES_DEV)
    return (owners * PAGES_DEV + local_page).reshape(QUERIES, CAND).astype(jnp.int32)


def place_ends(result, key, least, top_value):
    longest = result.shape.index(max(result.shape))
    spots = []
    for shift in (0, 1):
        where = [jax.random.randint(jax.random.fold_in(key, axis), (), 0, length) for axis, length in enumerate(result.shape)]
        where[longest] = (where[longest] + shift) % result.shape[longest]
        spots.append(tuple(where))
    return result.at[spots[0]].set(least).at[spots[1]].set(top_value)


def level_of(own_key, dims, shards, least, top_value):
    level, own = 1.0, jax.random.fold_in(own_key, 6)
    for axis_at, blocks in shards:
        heights = jnp.exp(jax.random.uniform(jax.random.fold_in(own, axis_at), (blocks,), jnp.float32, least / len(shards), top_value / len(shards)))
        level = level * jnp.repeat(heights, dims[axis_at] // blocks).reshape([-1 if axis == axis_at else 1 for axis in range(len(dims))])
    return level


def scatter_about(key, dims, scale, reach, shards=(), kind=jnp.bfloat16):
    result = jax.random.normal(key, dims, jnp.float32) * scale
    if len(shards) > 0:
        result = level_of(key, dims, shards, -0.22, 0.18) * result
    return jnp.clip(result, min=-reach, max=reach).astype(kind)


def setup_inputs(seed: int = 0, part: int = 0) -> dict:
    key_of = jax.random.split(jax.random.key(seed), 8)
    part_splits = jax.random.split(jax.random.fold_in(key_of[7], part), 8)
    return {
        "queries": scatter_about(part_splits[0], (QUERIES, DIN), 1.0, 6.0, ((0, 16),)),
        "rotation": scatter_about(key_of[1], (DIN, DIN), DIN ** -0.5, 0.1875, (), jnp.float32),
        "codes": scatter_about(part_splits[2], (PAGES, PAGE, DPROJ), DPROJ ** -0.5, 0.375, ((0, 16),)),
        "vectors": scatter_about(part_splits[3], (PAGES, PAGE, DIN), DIN ** -0.5, 0.1875, ((0, 16),), jnp.float32),
        "probes": draw_probes(jax.random.fold_in(jax.random.fold_in(key_of[7], part), 71), part),
        "cand_pages": draw_cand_pages(jax.random.fold_in(jax.random.fold_in(key_of[7], part), 71), part),
        "cand_rows": place_ends(jax.random.randint(part_splits[6], (QUERIES, CAND), 0, PAGE), jax.random.fold_in(part_splits[6], 1), 0, PAGE - 1).astype(jnp.int32),
    }


def reference(queries, rotation, codes, vectors, probes, cand_pages, cand_rows):
    rotated = jnp.dot(queries.astype(jnp.float32), rotation, precision=lax.Precision.HIGHEST, preferred_element_type=jnp.float32)
    projected = rotated[:, :DPROJ].astype(jnp.bfloat16)
    query_block_rows = projected.reshape(BLOCKS, QB, DPROJ)

    def score_block(inputs):
        queries_here, probe_list = inputs
        selected_entries = codes[probe_list].astype(jnp.float32)
        similarity_scores = jnp.einsum("qd,prd->qpr", queries_here.astype(jnp.float32), selected_entries, precision=lax.Precision.HIGHEST)
        return similarity_scores.astype(jnp.bfloat16)

    scored = lax.map(score_block, (query_block_rows, probes))
    coarse = scored.reshape(QUERIES, NPROBE * PAGE)
    gathered = vectors[cand_pages, cand_rows]
    rerank = jnp.einsum("qd,qcd->qc", rotated, gathered, precision=lax.Precision.HIGHEST)
    return coarse, rerank
```

```python
import functools

import jax
import jax.numpy as jnp
from jax import lax
from jax.experimental import pallas as pl
from jax.experimental.pallas import tpu as pltpu
from jax.sharding import PartitionSpec as P

LANES = 128
MIB = 1 << 20
F32, BF16, I32 = jnp.float32, jnp.bfloat16, jnp.int32
VMEM, SMEM, HBM = pltpu.VMEM, pltpu.SMEM, pl.ANY


def iota(shape, axis):
    return lax.broadcasted_iota(I32, shape, axis)


def dot(a, b, over_a=1, over_b=0):
    return lax.dot_general(a, b, (((over_a,), (over_b,)), ((), ())), preferred_element_type=F32)


def params(limit, **more):
    return pltpu.CompilerParams(vmem_limit_bytes=limit, **more)


def whole(space):
    return pl.BlockSpec(memory_space=space)


def thirds(x):
    high = x.astype(BF16)
    rest = x - high.astype(F32)
    middle = rest.astype(BF16)
    return high, middle, (rest - middle.astype(F32)).astype(BF16)


def rotate(queries, rotation):
    high, middle, low = thirds(rotation)
    return dot(queries, low) + dot(queries, middle) + dot(queries, high)


def owner_hot(owner, shards):
    cands = owner.shape[1]
    lanes = cands * shards
    spread = (iota((cands, lanes), 1) // shards == iota((cands, lanes), 0)).astype(BF16)
    wide = dot(owner.astype(BF16), spread)
    return (wide == (iota(wide.shape, 1) % shards).astype(F32)).astype(BF16), spread


def ranks(owner, shards):
    hot, spread = owner_hot(owner, shards)
    rows, lanes = hot.shape
    before = (iota((rows, rows), 1) < iota((rows, rows), 0)).astype(BF16)
    above = dot(before, hot)
    total = jnp.sum(hot.astype(F32), axis=0, keepdims=True)
    r, c = iota((lanes, lanes), 0), iota((lanes, lanes), 1)
    earlier = ((r % shards == c % shards) & (r // shards < c // shards)).astype(BF16)
    base = dot(jnp.broadcast_to(total, (8, lanes)).astype(BF16), earlier)[:1]
    rank = dot((hot.astype(F32) * (above + base)).astype(BF16), spread, 1, 1)
    return rank.astype(I32)


def plan_kernel(shards, page_count, q_ref, rot_ref, probes_ref, pages_ref, rows_ref, chunk_ref, probe_ref, place_ref):
    rows, cands = pages_ref.shape
    blocks, probes = probes_ref.shape
    chunk_ref[:rows, :] = rotate(q_ref[...], rot_ref[...]).astype(BF16)

    pages = pages_ref[...]
    owner = pages // page_count
    rank = ranks(owner, shards)
    place_ref[...] = jnp.concatenate([owner, rank], axis=1)
    local = (pages % page_count).astype(F32)
    line = rows_ref[...].astype(F32)

    lane = iota((rows, LANES), 1)
    kind, who = lane // shards, lane % shards
    query = iota((rows, LANES), 0).astype(F32)
    left, right = [], []
    for c in range(cands):
        value = jnp.where(kind == 0, query, jnp.where(kind == 1, local[:, c : c + 1], jnp.where(kind == 2, line[:, c : c + 1], 0.0)))
        left.append(jnp.where(owner[:, c : c + 1] == who, value, 0.0))
        right.append((rank[:, c : c + 1] == lane).astype(F32))
    table = dot(jnp.concatenate(left, 0).astype(BF16), jnp.concatenate(right, 0).astype(BF16), 0, 0)

    probe_pages = probes_ref[...]
    probe_owner = probe_pages // page_count
    probe_rank = ranks(probe_owner, shards)
    capacity = 2 * blocks * probes // shards
    probe_ref[...] = probe_owner * capacity + probe_rank
    value = (probe_pages % page_count + iota(probe_pages.shape, 0) * page_count).astype(F32)
    lane = iota((blocks, LANES), 1)
    kind, who = lane // shards, lane % shards
    left, right = [], []
    for c in range(probes):
        left.append(jnp.where((probe_owner[:, c : c + 1] == who) & (kind == 3), value[:, c : c + 1], 0.0))
        right.append((probe_rank[:, c : c + 1] == lane).astype(F32))
    table += dot(jnp.concatenate(left, 0).astype(BF16), jnp.concatenate(right, 0).astype(BF16), 0, 0)
    table = table.astype(BF16)
    chunk_ref[rows:, :LANES] = table[: 2 * shards]
    chunk_ref[rows:, LANES : 2 * LANES] = table[2 * shards : 4 * shards]


def rotate_kernel(q_ref, rot_ref, out_ref):
    out_ref[...] = rotate(q_ref[...], rot_ref[...]).astype(BF16)


def coarse_kernel(shards, capacity, block_rows, me_ref, *refs):
    pieces = refs[:shards]
    codes_ref, score_ref, line_ref, query_ref, slot_vec, slot_ref, sem = refs[shards:]
    page_count, page_rows, _ = codes_ref.shape
    me = me_ref[0]
    rows = pieces[0].shape[0] - 2 * shards
    mine = iota((shards, 1), 0) == me
    for m, piece in enumerate(pieces):
        first = jnp.sum(jnp.where(mine, piece[rows : rows + shards, :].astype(F32), 0.0), axis=0, keepdims=True).astype(I32)
        second = jnp.sum(jnp.where(mine, piece[rows + shards :, :].astype(F32), 0.0), axis=0, keepdims=True).astype(I32)
        query_ref[m : m + 1, :] = first[:, :LANES]
        line_ref[m : m + 1, :] = second[:, :LANES] * page_rows + first[:, LANES : 2 * LANES]
        slot_vec[m : m + 1, :] = second[:, LANES : 2 * LANES]
    copy = pltpu.make_async_copy(slot_vec, slot_ref, sem)
    copy.start()
    copy.wait()
    for m, piece in enumerate(pieces):
        source = me ^ m
        for s in range(capacity):
            slot = slot_ref[m, s]
            start = pl.multiple_of(slot // page_count * block_rows, block_rows)
            held = piece[pl.ds(start, block_rows), :]
            score_ref[source, s] = dot(held, codes_ref[slot % page_count], 1, 1).astype(BF16)


def gather_kernel(unroll, index_ref, vectors_ref, out_ref, sem):
    count = out_ref.shape[0]

    def issue(i, carry):
        for k in range(unroll):
            j = i * unroll + k
            row = index_ref[j // LANES, j % LANES]
            pltpu.make_async_copy(vectors_ref.at[pl.ds(row, 1)], out_ref.at[pl.ds(j, 1)], sem).start()
        return carry

    lax.fori_loop(0, count // unroll, issue, 0)
    pltpu.make_async_copy(vectors_ref.at[pl.ds(0, count)], out_ref, sem).wait()


def rerank_kernel(shards, capacity, me_ref, query_ref, rows_ref, *refs):
    heads, tails = refs[:shards], refs[shards : 2 * shards]
    out_ref, held, sems = refs[2 * shards :]
    me = me_ref[0]
    queries, split = tails[0].shape[0], heads[0].shape[1]
    copies = [
        pltpu.make_async_copy(rows_ref.at[pl.ds(m * capacity, capacity)], held.at[pl.ds(m * capacity, capacity)], sems.at[m])
        for m in range(shards)
    ]
    for copy in copies:
        copy.start()
    for m in range(shards):
        copies[m].wait()
        rows = held[m * capacity : (m + 1) * capacity, :]
        high = rows.astype(BF16)
        low = (rows - high.astype(F32)).astype(BF16)
        head, tail = heads[m][:queries, :], tails[m][...]
        score = dot(head, high[:, :split], 1, 1) + dot(tail, high[:, split:], 1, 1)
        score += dot(head, low[:, :split], 1, 1) + dot(tail, low[:, split:], 1, 1)
        picked = iota(score.shape, 0) == query_ref[m : m + 1, :capacity]
        out_ref[pl.ds(me ^ m, 1), :] = jnp.sum(jnp.where(picked, score, 0.0), axis=0, keepdims=True)


def pick_kernel(got_ref, place_ref, out_ref):
    shards, capacity = got_ref.shape
    rows, cands = out_ref.shape
    owner, rank = place_ref[:, :cands], place_ref[:, cands:]
    hot = jnp.concatenate(
        [(owner[:, c : c + 1] == iota((rows, shards), 1)).astype(F32) for c in range(cands)], axis=0
    ).astype(BF16)
    high, middle, low = thirds(got_ref[...])
    lines = dot(hot, low) + dot(hot, middle) + dot(hot, high)
    result = jnp.zeros((rows, cands), F32)
    for c in range(cands):
        here = jnp.where(rank[:, c : c + 1] == iota((rows, capacity), 1), lines[c * rows : (c + 1) * rows], 0.0)
        result = jnp.where(iota((rows, cands), 1) == c, jnp.sum(here, axis=1, keepdims=True), result)
    out_ref[...] = result


def place_kernel(place_ref, got_ref, out_ref):
    blocks, probes = place_ref.shape
    _, block_rows, page_rows = got_ref.shape
    for b in range(blocks):
        for p in range(probes):
            out_ref[b * block_rows : (b + 1) * block_rows, p * page_rows : (p + 1) * page_rows] = got_ref[place_ref[b, p]]


def exchange(x, mask, shards):
    return lax.ppermute(x, "idx", [(i, i ^ mask) for i in range(shards)])


def gather_all(x, shards):
    pieces = {0: x}
    for mask in range(4, shards, 4):
        pieces[mask] = exchange(x, mask, shards)
    for mask in range(0, shards, 4):
        pieces[mask ^ 2] = exchange(pieces[mask], 2, shards)
    for mask in range(0, shards, 2):
        pieces[mask ^ 1] = exchange(pieces[mask], 1, shards)
    return [pieces[m] for m in range(shards)]


def body(queries, rotation, codes, vectors, probes, cand_pages, cand_rows):
    shards = lax.axis_size("idx")
    me = lax.axis_index("idx").astype(I32).reshape(1)
    query_rows, full_width = queries.shape
    page_count, page_rows, proj_width = codes.shape
    block_count, probe_count = probes.shape
    block_rows = query_rows // block_count
    cand_count = cand_pages.shape[1]
    slot_count = block_count * probe_count
    capacity = 2 * slot_count // shards
    row_capacity = 2 * query_rows * cand_count // shards
    rest = full_width - proj_width
    assert proj_width == 2 * LANES and rest % proj_width == 0 and row_capacity <= LANES
    assert 4 * shards <= LANES and block_count * page_count <= 256 and query_rows <= 256 and page_rows <= 256

    chunk_rows = query_rows + 2 * shards
    chunk, probe_place, cand_place = pl.pallas_call(
        functools.partial(plan_kernel, shards, page_count),
        grid=(1,),
        in_specs=[
            pl.BlockSpec((query_rows, full_width), lambda i: (0, 0)),
            pl.BlockSpec((full_width, proj_width), lambda i: (0, 0)),
            pl.BlockSpec((block_count, probe_count), lambda i: (0, 0)),
            pl.BlockSpec((query_rows, cand_count), lambda i: (0, 0)),
            pl.BlockSpec((query_rows, cand_count), lambda i: (0, 0)),
        ],
        out_specs=[
            pl.BlockSpec((chunk_rows, proj_width), lambda i: (0, 0)),
            pl.BlockSpec((block_count, probe_count), lambda i: (0, 0)),
            pl.BlockSpec((query_rows, 2 * cand_count), lambda i: (0, 0)),
        ],
        out_shape=[
            jax.ShapeDtypeStruct((chunk_rows, proj_width), BF16),
            jax.ShapeDtypeStruct((block_count, probe_count), I32),
            jax.ShapeDtypeStruct((query_rows, 2 * cand_count), I32),
        ],
        compiler_params=params(32 * MIB),
        name="plan",
    )(queries, rotation, probes, cand_pages, cand_rows)
    tail = pl.pallas_call(
        rotate_kernel,
        grid=(rest // proj_width,),
        in_specs=[
            pl.BlockSpec((query_rows, full_width), lambda i: (0, 0)),
            pl.BlockSpec((full_width, proj_width), lambda i: (0, i + 1)),
        ],
        out_specs=pl.BlockSpec((query_rows, proj_width), lambda i: (0, i)),
        out_shape=jax.ShapeDtypeStruct((query_rows, rest), BF16),
        compiler_params=params(32 * MIB),
        name="rotate_rest",
    )(queries, rotation)

    heads = gather_all(chunk, shards)
    tails = gather_all(tail, shards)

    scored, lines, wanted = pl.pallas_call(
        functools.partial(coarse_kernel, shards, capacity, block_rows),
        in_specs=[whole(SMEM)] + [whole(VMEM)] * (shards + 1),
        out_specs=[whole(VMEM)] * 3,
        out_shape=[
            jax.ShapeDtypeStruct((shards, capacity, block_rows, page_rows), BF16),
            jax.ShapeDtypeStruct((shards, LANES), I32),
            jax.ShapeDtypeStruct((shards, LANES), I32),
        ],
        scratch_shapes=[pltpu.VMEM((shards, LANES), I32), pltpu.SMEM((shards, LANES), I32), pltpu.SemaphoreType.DMA],
        compiler_params=params(32 * MIB),
        name="coarse_scores",
    )(me, *heads, codes)
    returned = lax.all_to_all(scored, "idx", split_axis=0, concat_axis=0, tiled=True)

    flat = vectors.reshape(page_count * page_rows, full_width)
    line_list = lines[:, :row_capacity].reshape(-1, LANES)
    found = pl.pallas_call(
        functools.partial(gather_kernel, 16),
        in_specs=[whole(SMEM), whole(HBM)],
        out_specs=whole(HBM),
        out_shape=jax.ShapeDtypeStruct((shards * row_capacity, full_width), F32),
        scratch_shapes=[pltpu.SemaphoreType.DMA],
        compiler_params=params(32 * MIB),
        name="gather_rows",
    )(line_list, flat)

    answers = pl.pallas_call(
        functools.partial(rerank_kernel, shards, row_capacity),
        in_specs=[whole(SMEM), whole(VMEM), whole(HBM)] + [whole(VMEM)] * (2 * shards),
        out_specs=whole(VMEM),
        out_shape=jax.ShapeDtypeStruct((shards, row_capacity), F32),
        scratch_shapes=[pltpu.VMEM((shards * row_capacity, full_width), F32), pltpu.SemaphoreType.DMA((shards,))],
        compiler_params=params(48 * MIB),
        name="rerank_scores",
    )(me, wanted, found, *heads, *tails)
    answered = lax.all_to_all(answers, "idx", split_axis=0, concat_axis=0, tiled=True)

    rerank = pl.pallas_call(
        pick_kernel,
        in_specs=[whole(VMEM), whole(VMEM)],
        out_specs=whole(VMEM),
        out_shape=jax.ShapeDtypeStruct((query_rows, cand_count), F32),
        compiler_params=params(32 * MIB),
        name="pick_answers",
    )(answered, cand_place)
    coarse = pl.pallas_call(
        place_kernel,
        in_specs=[whole(SMEM), whole(VMEM)],
        out_specs=whole(VMEM),
        out_shape=jax.ShapeDtypeStruct((query_rows, probe_count * page_rows), BF16),
        compiler_params=params(32 * MIB),
        name="place_scores",
    )(probe_place, returned.reshape(shards * capacity, block_rows, page_rows))
    return coarse, rerank


def solution(mesh):
    split = P(("grp", "idx"))
    in_specs = (split, P(), split, split, split, split, split)
    return jax.shard_map(body, mesh=mesh, in_specs=in_specs, out_specs=(split, split), check_vma=False)
```

```python
import functools

import jax
import jax.numpy as jnp
from jax import lax
from jax.experimental import pallas as pl
from jax.experimental.pallas import tpu as pltpu
from jax.sharding import PartitionSpec as P

LANES = 128
MIB = 1 << 20
F32, BF16, I32 = jnp.float32, jnp.bfloat16, jnp.int32
VMEM, SMEM, HBM = pltpu.VMEM, pltpu.SMEM, pl.ANY


def iota(shape, axis):
    return lax.broadcasted_iota(I32, shape, axis)


def dot(a, b, over_a=1, over_b=0):
    return lax.dot_general(a, b, (((over_a,), (over_b,)), ((), ())), preferred_element_type=F32)


def params(limit, **more):
    return pltpu.CompilerParams(vmem_limit_bytes=limit, **more)


def whole(space):
    return pl.BlockSpec(memory_space=space)


def cost(us):
    return pl.CostEstimate(flops=0, bytes_accessed=us * 3_000_000, transcendentals=0)


def thirds(x):
    high = x.astype(BF16)
    rest = x - high.astype(F32)
    middle = rest.astype(BF16)
    return high, middle, (rest - middle.astype(F32)).astype(BF16)


def rotate(queries, rotation):
    high, middle, low = thirds(rotation)
    return dot(queries, low) + dot(queries, middle) + dot(queries, high)


def ranks(owner, shards):
    rows, lanes = owner.shape
    tall = rows * shards
    spread = (iota((tall, rows), 0) // shards == iota((tall, rows), 1)).astype(BF16)
    hot = (dot(spread, owner.astype(BF16)) == (iota((tall, lanes), 0) % shards).astype(F32)).astype(BF16)
    before = (iota((lanes, lanes), 0) < iota((lanes, lanes), 1)).astype(BF16)
    r, c = iota((tall, tall), 0), iota((tall, tall), 1)
    earlier = ((r % shards == c % shards) & (c // shards < r // shards)).astype(BF16)
    count = dot(hot, before) + jnp.sum(dot(earlier, hot), axis=1, keepdims=True)
    return dot(spread, (hot.astype(F32) * count).astype(BF16), 0, 0).astype(I32)


def table_part(owner, rank, values, shards, kinds):
    rows, lanes = owner.shape
    line = iota((LANES, lanes), 0)
    kind, who = line // shards, line % shards
    left, right = [], []
    for c in range(rows):
        value = jnp.zeros((LANES, lanes), F32)
        for k, v in zip(kinds, values, strict=True):
            value = jnp.where(kind == k, v[c : c + 1], value)
        left.append(jnp.where(owner[c : c + 1] == who, value, 0.0))
        right.append((rank[c : c + 1] == line).astype(F32))
    total = jnp.zeros((LANES, LANES), F32)
    if lanes % LANES == 0:
        return dot(jnp.concatenate(left, 1).astype(BF16), jnp.concatenate(right, 1).astype(BF16), 1, 1)
    for l, r in zip(left, right, strict=True):
        total += dot(l.astype(BF16), r.astype(BF16), 1, 1)
    return total


def plan_kernel(shards, page_count, q_ref, rot_ref, probes_ref, pages_ref, rows_ref, chunk_ref, probe_ref, place_ref, held, sem):
    cands, rows = pages_ref.shape
    blocks, probes = probes_ref.shape
    copy = pltpu.make_async_copy(rot_ref.at[:, pl.ds(0, held.shape[1])], held, sem)
    copy.start()
    pages = pages_ref[...]
    owner = pages // page_count
    rank = ranks(owner, shards)
    place_ref[:cands] = owner
    place_ref[cands:] = rank
    query = iota((cands, rows), 1).astype(F32)
    values = (query, (pages % page_count).astype(F32), rows_ref[...].astype(F32))
    table = table_part(owner, rank, values, shards, (0, 1, 2))

    probe_pages = probes_ref[...]
    probe_owner = probe_pages // page_count
    probe_rank = ranks(probe_owner, shards)
    probe_ref[...] = probe_owner * (2 * blocks * probes // shards) + probe_rank
    value = (probe_pages % page_count + iota(probe_pages.shape, 0) * page_count).astype(F32)
    table += table_part(probe_owner, probe_rank, (value,), shards, (3,))
    table = table.astype(BF16)
    chunk_ref[rows:, :LANES] = table[: 2 * shards]
    chunk_ref[rows:, LANES : 2 * LANES] = table[2 * shards : 4 * shards]
    copy.wait()
    chunk_ref[:rows, :] = rotate(q_ref[...], held[...]).astype(BF16)


def rotate_kernel(q_ref, rot_ref, out_ref):
    out_ref[...] = rotate(q_ref[...], rot_ref[...]).astype(BF16)


def coarse_kernel(shards, capacity, block_rows, me_ref, *refs):
    parts = refs[:shards]
    codes_ref, score_ref, line_ref, query_ref, held, slot_vec, slot_ref, sems, sem = refs[shards:]
    page_count, page_rows, _ = codes_ref.shape
    me = me_ref[0]
    rows = held.shape[1] - 2 * shards
    loads = [pltpu.make_async_copy(part, held.at[m], sems.at[m]) for m, part in enumerate(parts)]
    for load in loads:
        load.start()
    mine = iota((shards, 1), 0) == me
    for m in range(shards):
        loads[m].wait()
        first = jnp.sum(jnp.where(mine, held[m, rows : rows + shards, :].astype(F32), 0.0), axis=0, keepdims=True).astype(I32)
        second = jnp.sum(jnp.where(mine, held[m, rows + shards :, :].astype(F32), 0.0), axis=0, keepdims=True).astype(I32)
        line = second[:, :LANES] * page_rows + first[:, LANES : 2 * LANES]
        query_ref[m : m + 1, :] = first[:, :LANES]
        line_ref[m : m + 1, :] = line
        slot_vec[m : m + 1, :] = second[:, LANES : 2 * LANES]
    copy = pltpu.make_async_copy(slot_vec, slot_ref, sem)
    copy.start()
    copy.wait()
    for m in range(shards):
        source = me ^ m
        for s in range(capacity):
            slot = slot_ref[m, s]
            start = pl.multiple_of(slot // page_count * block_rows, block_rows)
            score_ref[source, s] = dot(held[m, pl.ds(start, block_rows), :], codes_ref[slot % page_count], 1, 1).astype(BF16)


def gather_kernel(shards, capacity, index_ref, lines_ref, out_ref, lines, picked, sems, out_sem):
    tiles = out_ref.shape[2] // LANES
    parts = sems.shape[0]
    size = lines.shape[0] // parts
    loads = [
        pltpu.make_async_copy(lines_ref.at[pl.ds(i * size, size)], lines.at[pl.ds(i * size, size)], sems.at[i])
        for i in range(parts)
    ]
    for load in loads:
        load.start()
    for load in loads:
        load.wait()

    @pl.loop(0, shards)
    def _(m):
        for j in range(capacity):
            row = index_ref[m, j]
            start = (row // 8) * (8 * tiles) + row % 8
            picked[pl.ds(j // 8 * 8 * tiles + j % 8, tiles, stride=8), :] = lines[pl.ds(start, tiles, stride=8), :]
        for k in range(tiles):
            for g in range(0, capacity, 16):
                pair = [picked[(g + h) * tiles + k * 8 : (g + h) * tiles + k * 8 + 8, :] for h in (0, 8)]
                part = jnp.concatenate(pair, axis=0)
                high = part.astype(BF16)
                out_ref[m, g : g + 16, k * LANES : (k + 1) * LANES] = high
                low = (part - high.astype(F32)).astype(BF16)
                out_ref[m, capacity + g : capacity + g + 16, k * LANES : (k + 1) * LANES] = low


def rerank_kernel(shards, capacity, me_ref, query_ref, rows_ref, *refs):
    heads, tails = refs[:shards], refs[shards : 2 * shards]
    outs = refs[2 * shards : 2 * shards + shards // 4]
    rows, head, tail, sems = refs[2 * shards + shards // 4 :]
    queries, split = head.shape[1:]
    copies = [
        (
            pltpu.make_async_copy(rows_ref.at[m], rows.at[m], sems.at[m, 0]),
            pltpu.make_async_copy(heads[m].at[pl.ds(0, queries)], head.at[m], sems.at[m, 1]),
            pltpu.make_async_copy(tails[m], tail.at[m], sems.at[m, 2]),
        )
        for m in range(shards)
    ]
    for trio in copies:
        for copy in trio:
            copy.start()
    for m in range(shards):
        for copy in copies[m]:
            copy.wait()
        score = dot(head[m], rows[m, :, :split], 1, 1) + dot(tail[m], rows[m, :, split:], 1, 1)
        score = score[:, :capacity] + score[:, capacity:]
        picked = iota(score.shape, 0) == query_ref[m : m + 1, :capacity]
        outs[m // 4][m % 4 : m % 4 + 1, :] = jnp.sum(jnp.where(picked, score, 0.0), axis=0, keepdims=True)


def pick_kernel(shards, me_ref, own_ref, y_ref, core_ref, both_ref, place_ref, out_ref, got):
    cands, rows = out_ref.shape
    capacity = got.shape[1]
    for a in range(shards // 4):
        for low, ref in enumerate((own_ref, core_ref, y_ref, both_ref)):
            got[4 * a + low : 4 * a + low + 1, :] = ref[a, low : low + 1, :]
    piece, rank = place_ref[:cands] ^ me_ref[0], place_ref[cands:]
    hot = [(piece[c : c + 1] == iota((shards, rows), 0)).astype(F32) for c in range(cands)]
    hot = jnp.concatenate(hot, axis=1).astype(BF16)
    high, middle, low = thirds(got[...])
    lines = dot(low, hot, 0, 0) + dot(middle, hot, 0, 0) + dot(high, hot, 0, 0)
    for c in range(cands):
        here = rank[c : c + 1] == iota((capacity, rows), 0)
        out_ref[c : c + 1, :] = jnp.sum(jnp.where(here, lines[:, c * rows : (c + 1) * rows], 0.0), axis=0, keepdims=True)


def place_kernel(place_ref, got_ref, out_ref):
    blocks, probes = place_ref.shape
    _, block_rows, page_rows = got_ref.shape
    for b in range(blocks):
        for p in range(probes):
            out_ref[b * block_rows : (b + 1) * block_rows, p * page_rows : (p + 1) * page_rows] = got_ref[place_ref[b, p]]


def exchange(x, mask, shards):
    return lax.ppermute(x, "idx", [(i, i ^ mask) for i in range(shards)])


def gather_all(x, shards):
    pieces = {0: x}
    for mask in range(4, shards, 4):
        pieces[mask] = exchange(x, mask, shards)
    for mask in range(0, shards, 4):
        pieces[mask ^ 2] = exchange(pieces[mask], 2, shards)
    for mask in range(0, shards, 2):
        pieces[mask ^ 1] = exchange(pieces[mask], 1, shards)
    return [pieces[m] for m in range(shards)]


def body(queries, rotation, codes, vectors, probes, cand_pages, cand_rows):
    shards = lax.axis_size("idx")
    me = lax.axis_index("idx").astype(I32).reshape(1)
    query_rows, full_width = queries.shape
    page_count, page_rows, proj_width = codes.shape
    block_count, probe_count = probes.shape
    block_rows = query_rows // block_count
    cand_count = cand_pages.shape[1]
    slot_count = block_count * probe_count
    capacity = 2 * slot_count // shards
    row_capacity = 2 * query_rows * cand_count // shards
    rest = full_width - proj_width
    assert proj_width == 2 * LANES and rest % proj_width == 0 and row_capacity <= LANES
    assert 4 * shards <= LANES and block_count * page_count <= 256 and query_rows <= 256 and page_rows <= 256

    chunk_rows = query_rows + 2 * shards
    chunk, probe_place, cand_place = pl.pallas_call(
        functools.partial(plan_kernel, shards, page_count),
        in_specs=[whole(VMEM), whole(HBM), whole(VMEM), whole(VMEM), whole(VMEM)],
        out_specs=[whole(VMEM)] * 3,
        out_shape=[
            jax.ShapeDtypeStruct((chunk_rows, proj_width), BF16),
            jax.ShapeDtypeStruct((block_count, probe_count), I32),
            jax.ShapeDtypeStruct((2 * cand_count, query_rows), I32),
        ],
        scratch_shapes=[pltpu.VMEM((full_width, proj_width), F32), pltpu.SemaphoreType.DMA],
        compiler_params=params(32 * MIB),
        cost_estimate=cost(2),
        name="plan",
    )(queries, rotation, probes, cand_pages.T, cand_rows.T)
    tail = pl.pallas_call(
        rotate_kernel,
        grid=(rest // proj_width,),
        in_specs=[
            pl.BlockSpec((query_rows, full_width), lambda i: (0, 0)),
            pl.BlockSpec((full_width, proj_width), lambda i: (0, i + 1)),
        ],
        out_specs=pl.BlockSpec((query_rows, proj_width), lambda i: (0, i)),
        out_shape=jax.ShapeDtypeStruct((query_rows, rest), BF16),
        compiler_params=params(32 * MIB),
        cost_estimate=cost(2),
        name="rotate_rest",
    )(queries, rotation)

    heads = gather_all(chunk, shards)
    tails = gather_all(tail, shards)

    scored, lines, wanted = pl.pallas_call(
        functools.partial(coarse_kernel, shards, capacity, block_rows),
        in_specs=[whole(SMEM)] + [whole(HBM)] * shards + [whole(VMEM)],
        out_specs=[whole(VMEM)] * 3,
        out_shape=[
            jax.ShapeDtypeStruct((shards, capacity, block_rows, page_rows), BF16),
            jax.ShapeDtypeStruct((shards, LANES), I32),
            jax.ShapeDtypeStruct((shards, LANES), I32),
        ],
        scratch_shapes=[
            pltpu.VMEM((shards, chunk_rows, proj_width), BF16),
            pltpu.VMEM((shards, LANES), I32),
            pltpu.SMEM((shards, LANES), I32),
            pltpu.SemaphoreType.DMA((shards,)),
            pltpu.SemaphoreType.DMA,
        ],
        compiler_params=params(32 * MIB),
        cost_estimate=cost(6),
        name="coarse_scores",
    )(me, *heads, codes)
    returned = lax.all_to_all(scored, "idx", split_axis=0, concat_axis=0, tiled=True)

    tiles = full_width // LANES
    flat = vectors.reshape(page_count * page_rows // 8, 8, tiles, LANES).transpose(0, 2, 1, 3).reshape(-1, LANES)
    found = pl.pallas_call(
        functools.partial(gather_kernel, shards, row_capacity),
        in_specs=[whole(SMEM), whole(HBM)],
        out_specs=whole(VMEM),
        out_shape=jax.ShapeDtypeStruct((shards, 2 * row_capacity, full_width), BF16),
        scratch_shapes=[
            pltpu.VMEM(flat.shape, F32),
            pltpu.VMEM((row_capacity * tiles, LANES), F32),
            pltpu.SemaphoreType.DMA((4,)),
            pltpu.SemaphoreType.DMA,
        ],
        compiler_params=params(48 * MIB),
        cost_estimate=cost(15),
        name="gather_rows",
    )(lines, flat)

    answers = pl.pallas_call(
        functools.partial(rerank_kernel, shards, row_capacity),
        in_specs=[whole(SMEM), whole(VMEM), whole(HBM)] + [whole(HBM)] * (2 * shards),
        out_specs=[whole(VMEM)] * (shards // 4),
        out_shape=[jax.ShapeDtypeStruct((4, row_capacity), F32)] * (shards // 4),
        scratch_shapes=[
            pltpu.VMEM((shards, 2 * row_capacity, full_width), BF16),
            pltpu.VMEM((shards, query_rows, proj_width), BF16),
            pltpu.VMEM((shards, query_rows, rest), BF16),
            pltpu.SemaphoreType.DMA((shards, 3)),
        ],
        compiler_params=params(48 * MIB),
        cost_estimate=cost(8),
        name="rerank_scores",
    )(me, wanted, found, *heads, *tails)
    own = jnp.stack([answers[0]] + [exchange(answers[a], 4 * a, shards) for a in range(1, shards // 4)])
    across = exchange(own, 2, shards)
    rerank = pl.pallas_call(
        functools.partial(pick_kernel, shards),
        in_specs=[whole(SMEM)] + [whole(VMEM)] * 5,
        out_specs=whole(VMEM),
        out_shape=jax.ShapeDtypeStruct((cand_count, query_rows), F32),
        scratch_shapes=[pltpu.VMEM((shards, row_capacity), F32)],
        compiler_params=params(32 * MIB),
        cost_estimate=cost(1),
        name="pick_answers",
    )(me, own, across, exchange(own, 1, shards), exchange(across, 1, shards), cand_place).T
    coarse = pl.pallas_call(
        place_kernel,
        in_specs=[whole(SMEM), whole(VMEM)],
        out_specs=whole(VMEM),
        out_shape=jax.ShapeDtypeStruct((query_rows, probe_count * page_rows), BF16),
        compiler_params=params(32 * MIB),
        cost_estimate=cost(1),
        name="place_scores",
    )(probe_place, returned.reshape(shards * capacity, block_rows, page_rows))
    return coarse, rerank


def solution(mesh):
    split = P(("grp", "idx"))
    in_specs = (split, P(), split, split, split, split, split)
    return jax.shard_map(body, mesh=mesh, in_specs=in_specs, out_specs=(split, split), check_vma=False)
```

```python
import functools

import jax
import jax.numpy as jnp
from jax import lax
from jax.experimental import pallas as pl
from jax.experimental.pallas import tpu as pltpu
from jax.sharding import PartitionSpec as P

LANES = 128
MIB = 1 << 20
COARSE_COST, GATHER_COST, RERANK_COST = 3, 12, 1
F32, BF16, I32 = jnp.float32, jnp.bfloat16, jnp.int32
VMEM, SMEM, HBM, ANY = pltpu.VMEM, pltpu.SMEM, pltpu.HBM, pl.ANY


def iota(shape, axis):
    return lax.broadcasted_iota(I32, shape, axis)


def dot(a, b, over_a=1, over_b=0):
    return lax.dot_general(a, b, (((over_a,), (over_b,)), ((), ())), preferred_element_type=F32)


def params(limit, **more):
    return pltpu.CompilerParams(vmem_limit_bytes=limit, **more)


def whole(space):
    return pl.BlockSpec(memory_space=space)


def cost(us):
    return pl.CostEstimate(flops=0, bytes_accessed=us * 3_000_000, transcendentals=0)


def parts_of(x, count):
    parts = []
    for _ in range(count):
        parts.append(x.astype(BF16))
        x = x - parts[-1].astype(F32)
    return parts


def rotate(queries, rotation):
    high, low = parts_of(rotation, 2)
    return dot(queries, low) + dot(queries, high)


def ranks(owner, shards):
    rows, lanes = owner.shape
    tall = rows * shards
    spread = (iota((tall, rows), 0) // shards == iota((tall, rows), 1)).astype(BF16)
    hot = (dot(spread, owner.astype(BF16)) == (iota((tall, lanes), 0) % shards).astype(F32)).astype(BF16)
    before = (iota((lanes, lanes), 0) < iota((lanes, lanes), 1)).astype(BF16)
    r, c = iota((tall, tall), 0), iota((tall, tall), 1)
    earlier = ((r % shards == c % shards) & (c // shards < r // shards)).astype(BF16)
    count = dot(hot, before) + jnp.sum(dot(earlier, hot), axis=1, keepdims=True)
    return dot(spread, (hot.astype(F32) * count).astype(BF16), 0, 0).astype(I32)


def table_part(owner, rank, values, shards, kinds):
    rows, lanes = owner.shape
    line = iota((LANES, lanes), 0)
    kind, who = line // shards, line % shards
    left, right = [], []
    for c in range(rows):
        value = jnp.zeros((LANES, lanes), F32)
        for k, v in zip(kinds, values, strict=True):
            value = jnp.where(kind == k, v[c : c + 1], value)
        left.append(jnp.where(owner[c : c + 1] == who, value, 0.0))
        right.append((rank[c : c + 1] == line).astype(F32))
    total = jnp.zeros((LANES, LANES), F32)
    if lanes % LANES == 0:
        return dot(jnp.concatenate(left, 1).astype(BF16), jnp.concatenate(right, 1).astype(BF16), 1, 1)
    for l, r in zip(left, right, strict=True):
        total += dot(l.astype(BF16), r.astype(BF16), 1, 1)
    return total


def plan_kernel(shards, page_count, q_hbm, rot_hbm, probes_hbm, pages_hbm, rows_hbm, chunk_ref, tail_ref, probe_ref, place_ref, q_ref, held, probes_ref, pages_ref, rows_ref, sems):
    cands, rows = pages_ref.shape
    blocks, probes = probes_ref.shape
    width = chunk_ref.shape[1]
    count = held.shape[0]
    pairs = [(pages_hbm, pages_ref), (rows_hbm, rows_ref), (probes_hbm, probes_ref), (q_hbm, q_ref)]
    pairs += [(rot_hbm.at[:, pl.ds(i * width, width)], held.at[i]) for i in range(count)]
    copies = [pltpu.make_async_copy(source, target, sems.at[i]) for i, (source, target) in enumerate(pairs)]
    for copy in copies:
        copy.start()
    for copy in copies[:3]:
        copy.wait()
    pages = pages_ref[...]
    owner = pages // page_count
    rank = ranks(owner, shards)
    place_ref[:cands] = owner
    place_ref[cands:] = rank
    query = iota((cands, rows), 1).astype(F32)
    values = (query, (pages % page_count).astype(F32), rows_ref[...].astype(F32))
    table = table_part(owner, rank, values, shards, (0, 1, 2))

    probe_pages = probes_ref[...]
    probe_owner = probe_pages // page_count
    probe_rank = ranks(probe_owner, shards)
    probe_ref[...] = probe_owner * (2 * blocks * probes // shards) + probe_rank
    value = (probe_pages % page_count + iota(probe_pages.shape, 0) * page_count).astype(F32)
    table += table_part(probe_owner, probe_rank, (value,), shards, (3,))
    table = table.astype(BF16)
    chunk_ref[rows:, :LANES] = table[: 2 * shards]
    chunk_ref[rows:, LANES : 2 * LANES] = table[2 * shards : 4 * shards]
    copies[3].wait()
    for i in range(count):
        copies[4 + i].wait()
        part = rotate(q_ref[...], held[i]).astype(BF16)
        if i == 0:
            chunk_ref[:rows, :] = part
        else:
            tail_ref[:, (i - 1) * width : i * width] = part


def stack_kernel(others, *refs):
    *parts, out_ref = refs[others:]
    for i, part in enumerate(parts):
        out_ref[i] = part[...]


def coarse_kernel(shards, order, block_rows, me_ref, pieces, codes, *refs):
    score_ref, list_ref, lists, slots, slot_ref, sems = refs[-6:]
    capacity = score_ref.shape[1]
    page_count, page_rows, _ = codes.shape
    me = me_ref[0]
    rows = pieces.shape[1] - 2 * shards
    mine = iota((shards, 1), 0) == me
    for p in range(len(order)):
        first = jnp.sum(jnp.where(mine, pieces[p, rows : rows + shards, :].astype(F32), 0.0), axis=0, keepdims=True).astype(I32)
        second = jnp.sum(jnp.where(mine, pieces[p, rows + shards :, :].astype(F32), 0.0), axis=0, keepdims=True).astype(I32)
        lists[0, p : p + 1, :] = second[:, :LANES] * page_rows + first[:, LANES : 2 * LANES]
        lists[1, p : p + 1, :] = first[:, :LANES]
        slots[p : p + 1, :] = second[:, LANES : 2 * LANES]
    copy = pltpu.make_async_copy(slots, slot_ref, sems.at[0])
    copy.start()
    save = pltpu.make_async_copy(lists, list_ref, sems.at[1])
    save.start()
    copy.wait()
    for p, piece in enumerate(order):
        source = me ^ piece
        for s in range(capacity):
            slot = slot_ref[p, s]
            start = pl.multiple_of(slot // page_count * block_rows, block_rows)
            score_ref[source, s] = dot(pieces[p, pl.ds(start, block_rows), :], codes[slot % page_count], 1, 1).astype(BF16)
    save.wait()


def gather_kernel(list_a, list_b, lines_hbm, out_ref, index_ref, lines, sems):
    _, half, capacity, width = out_ref.shape
    count = sems.shape[0] - 2
    size = lines.shape[0] // count
    loads = [
        pltpu.make_async_copy(lines_hbm.at[pl.ds(i * size, size)], lines.at[pl.ds(i * size, size)], sems.at[i])
        for i in range(count)
    ]
    loads.append(pltpu.make_async_copy(list_a.at[0], index_ref.at[pl.ds(0, half)], sems.at[count]))
    loads.append(pltpu.make_async_copy(list_b.at[0], index_ref.at[pl.ds(half, half)], sems.at[count + 1]))
    for load in loads:
        load.start()
    for load in loads:
        load.wait()
    sublane = iota((8, width), 0)

    @pl.loop(0, 2 * half)
    def _(m):
        for g in range(0, capacity, 16):
            halves = []
            for h in range(g, g + 16, 8):
                eight = jnp.zeros((8, width), F32)
                for j in range(8):
                    row = jnp.broadcast_to(lines[pl.ds(index_ref[m, h + j], 1), :], (8, width))
                    eight = jnp.where(sublane == j, row, eight)
                halves.append(eight)
            out_ref[m // half, m % half, g : g + 16, :] = jnp.concatenate(halves, axis=0).astype(BF16)


def rerank_kernel(part, order, list_ref, rows_ref, heads_ref, tails_ref, *refs):
    *before, out_ref, query_ref, sem = refs
    capacity = rows_ref.shape[2]
    queries, split = tails_ref.shape[1], heads_ref.shape[2]
    copy = pltpu.make_async_copy(list_ref.at[1], query_ref, sem)
    copy.start()
    if before:
        out_ref[...] = before[0][...]
    copy.wait()
    for p, m in enumerate(order):
        score = dot(heads_ref[p, :queries, :], rows_ref[part, p, :, :split], 1, 1)
        score += dot(tails_ref[p], rows_ref[part, p, :, split:], 1, 1)
        picked = iota(score.shape, 0) == query_ref[p : p + 1, :capacity]
        out_ref[m // 4, m % 4 : m % 4 + 1, :] = jnp.sum(jnp.where(picked, score, 0.0), axis=0, keepdims=True)


def pick_kernel(shards, me_ref, own_ref, y_ref, core_ref, both_ref, place_ref, out_ref, got):
    cands, rows = out_ref.shape
    capacity = got.shape[1]
    for a in range(shards // 4):
        for low, ref in enumerate((own_ref, core_ref, y_ref, both_ref)):
            got[4 * a + low : 4 * a + low + 1, :] = ref[a, low : low + 1, :]
    piece, rank = place_ref[:cands] ^ me_ref[0], place_ref[cands:]
    hot = [(piece[c : c + 1] == iota((shards, rows), 0)).astype(F32) for c in range(cands)]
    hot = jnp.concatenate(hot, axis=1).astype(BF16)
    high, middle, low = parts_of(got[...], 3)
    lines = dot(low, hot, 0, 0) + dot(middle, hot, 0, 0) + dot(high, hot, 0, 0)
    for c in range(cands):
        here = rank[c : c + 1] == iota((capacity, rows), 0)
        out_ref[c : c + 1, :] = jnp.sum(jnp.where(here, lines[:, c * rows : (c + 1) * rows], 0.0), axis=0, keepdims=True)


def place_kernel(place_ref, got_ref, out_ref):
    blocks, probes = place_ref.shape
    _, block_rows, page_rows = got_ref.shape
    for b in range(blocks):
        for p in range(probes):
            out_ref[b * block_rows : (b + 1) * block_rows, p * page_rows : (p + 1) * page_rows] = got_ref[place_ref[b, p]]


def exchange(x, mask, shards):
    return lax.ppermute(x, "idx", [(i, i ^ mask) for i in range(shards)])


def planes(x, shards):
    along = {mask: exchange(x, mask, shards) if mask else x for mask in range(0, shards, 4)}
    return along, lambda: {mask ^ 2: exchange(along[mask], 2, shards) for mask in along}


def body(queries, rotation, codes, vectors, probes, cand_pages, cand_rows):
    shards = lax.axis_size("idx")
    me = lax.axis_index("idx").astype(I32).reshape(1)
    query_rows, full_width = queries.shape
    page_count, page_rows, proj_width = codes.shape
    block_count, probe_count = probes.shape
    block_rows = query_rows // block_count
    cand_count = cand_pages.shape[1]
    slot_count = block_count * probe_count
    capacity = 2 * slot_count // shards
    row_capacity = 2 * query_rows * cand_count // shards
    rest = full_width - proj_width
    assert proj_width == 2 * LANES and rest % proj_width == 0 and row_capacity <= LANES
    assert 4 * shards <= LANES and block_count * page_count <= 256 and query_rows <= 256 and page_rows <= 256

    chunk_rows = query_rows + 2 * shards
    chunk, tail, probe_place, cand_place = pl.pallas_call(
        functools.partial(plan_kernel, shards, page_count),
        in_specs=[whole(HBM)] * 5,
        out_specs=[whole(VMEM)] * 4,
        out_shape=[
            jax.ShapeDtypeStruct((chunk_rows, proj_width), BF16),
            jax.ShapeDtypeStruct((query_rows, rest), BF16),
            jax.ShapeDtypeStruct((block_count, probe_count), I32),
            jax.ShapeDtypeStruct((2 * cand_count, query_rows), I32),
        ],
        scratch_shapes=[
            pltpu.VMEM(queries.shape, BF16),
            pltpu.VMEM((full_width // proj_width, full_width, proj_width), F32),
            pltpu.VMEM(probes.shape, I32),
            pltpu.VMEM((cand_count, query_rows), I32),
            pltpu.VMEM((cand_count, query_rows), I32),
            pltpu.SemaphoreType.DMA((4 + full_width // proj_width,)),
        ],
        compiler_params=params(61 * MIB),
        cost_estimate=cost(2),
        name="plan",
    )(queries, rotation, probes, cand_pages.T, cand_rows.T)
    order = tuple(range(0, shards, 2))
    other = tuple(m ^ 1 for m in order)

    def stack(parts, waits, name):
        return pl.pallas_call(
            functools.partial(stack_kernel, len(waits)),
            in_specs=[whole(ANY)] * len(waits) + [whole(VMEM)] * len(parts),
            out_specs=whole(VMEM),
            out_shape=jax.ShapeDtypeStruct((len(parts), *parts[0].shape), BF16),
            compiler_params=params(10 * MIB),
            cost_estimate=cost(1),
            name=name,
        )(*waits, *parts)

    def coarse_scores(order, pieces, waits, before):
        count = 3 + len(waits)
        return pl.pallas_call(
            functools.partial(coarse_kernel, shards, order, block_rows),
            in_specs=[whole(SMEM), whole(VMEM), whole(VMEM)] + [whole(ANY)] * len(waits) + [whole(VMEM)] * len(before),
            out_specs=[whole(VMEM), whole(ANY)],
            out_shape=[
                jax.ShapeDtypeStruct((shards, capacity, block_rows, page_rows), BF16),
                jax.ShapeDtypeStruct((2, len(order), LANES), I32),
            ],
            scratch_shapes=[
                pltpu.VMEM((2, len(order), LANES), I32),
                pltpu.VMEM((len(order), LANES), I32),
                pltpu.SMEM((len(order), LANES), I32),
                pltpu.SemaphoreType.DMA((2,)),
            ],
            input_output_aliases={count: 0} if before else {},
            compiler_params=params(10 * MIB),
            cost_estimate=cost(COARSE_COST),
            name="coarse_scores",
        )(me, pieces, codes, *waits, *before)

    along, across = planes(chunk, shards)
    plane = along | across()
    tail_along = {mask: exchange(tail, mask, shards) for mask in range(4, shards, 4)}
    tail_across = {2: exchange(tail, 2, shards)}

    heads_a = stack([plane[m] for m in order], list(tail_along.values()), "stack_heads")
    heads_b = exchange(heads_a, 1, shards)
    scored, list_a = coarse_scores(order, heads_a, [], [])
    scored, list_b = coarse_scores(other, heads_b, [], [scored])
    returned = lax.all_to_all(scored, "idx", split_axis=0, concat_axis=0, tiled=True)

    tail_across |= {mask ^ 2: exchange(x, 2, shards) for mask, x in tail_along.items()}
    tails = {0: tail} | tail_along | tail_across

    flat = vectors.reshape(page_count * page_rows, full_width)
    found = pl.pallas_call(
        gather_kernel,
        in_specs=[whole(ANY)] * 3,
        out_specs=whole(VMEM),
        out_shape=jax.ShapeDtypeStruct((2, len(order), row_capacity, full_width), BF16),
        scratch_shapes=[
            pltpu.SMEM((shards, LANES), I32),
            pltpu.VMEM(flat.shape, F32),
            pltpu.SemaphoreType.DMA((6,)),
        ],
        compiler_params=params(34 * MIB),
        cost_estimate=cost(GATHER_COST),
        name="gather_rows",
    )(list_a, list_b, flat)
    tails_a = stack([tails[m] for m in order], [found], "stack_tails")
    tails_b = exchange(tails_a, 1, shards)

    def scores(part, order, list_ref, heads, tails, before):
        return pl.pallas_call(
            functools.partial(rerank_kernel, part, order),
            in_specs=[whole(ANY)] + [whole(VMEM)] * (3 + len(before)),
            out_specs=whole(VMEM),
            out_shape=jax.ShapeDtypeStruct((shards // 4, 4, row_capacity), F32),
            scratch_shapes=[pltpu.VMEM((len(order), LANES), I32), pltpu.SemaphoreType.DMA],
            compiler_params=params(10 * MIB),
            cost_estimate=cost(RERANK_COST),
            name="rerank_scores",
        )(list_ref, found, heads, tails, *before)

    answers = scores(0, order, list_a, heads_a, tails_a, [])
    answers = scores(1, other, list_b, heads_b, tails_b, [answers])
    own = jnp.stack([exchange(answers[a], 4 * a, shards) if a else answers[a] for a in range(shards // 4)])
    across = exchange(own, 2, shards)
    coarse = pl.pallas_call(
        place_kernel,
        in_specs=[whole(SMEM), whole(VMEM)],
        out_specs=whole(VMEM),
        out_shape=jax.ShapeDtypeStruct((query_rows, probe_count * page_rows), BF16),
        compiler_params=params(10 * MIB),
        cost_estimate=cost(1),
        name="place_scores",
    )(probe_place, returned.reshape(shards * capacity, block_rows, page_rows))
    rerank = pl.pallas_call(
        functools.partial(pick_kernel, shards),
        in_specs=[whole(SMEM)] + [whole(VMEM)] * 5,
        out_specs=whole(VMEM),
        out_shape=jax.ShapeDtypeStruct((cand_count, query_rows), F32),
        scratch_shapes=[pltpu.VMEM((shards, row_capacity), F32)],
        compiler_params=params(10 * MIB),
        cost_estimate=cost(1),
        name="pick_answers",
    )(me, own, across, exchange(own, 1, shards), exchange(across, 1, shards), cand_place).T
    return coarse, rerank


def solution(mesh):
    split = P(("grp", "idx"))
    in_specs = (split, P(), split, split, split, split, split)
    return jax.shard_map(body, mesh=mesh, in_specs=in_specs, out_specs=(split, split), check_vma=False)
```

```python
import functools

import jax
import jax.numpy as jnp
from jax import lax
from jax.experimental import pallas as pl
from jax.experimental.pallas import tpu as pltpu
from jax.sharding import PartitionSpec as P

LANES = 128
MIB = 1 << 20
TAIL_MIB = 58
COARSE_COST, GATHER_COST, RERANK_COST = 3, 12, 1
F32, BF16, I32 = jnp.float32, jnp.bfloat16, jnp.int32
VMEM, SMEM, HBM, ANY = pltpu.VMEM, pltpu.SMEM, pltpu.HBM, pl.ANY


def iota(shape, axis):
    return lax.broadcasted_iota(I32, shape, axis)


def dot(a, b, over_a=1, over_b=0):
    return lax.dot_general(a, b, (((over_a,), (over_b,)), ((), ())), preferred_element_type=F32)


def params(limit, **more):
    return pltpu.CompilerParams(vmem_limit_bytes=limit, **more)


def whole(space):
    return pl.BlockSpec(memory_space=space)


def cost(us):
    return pl.CostEstimate(flops=0, bytes_accessed=us * 3_000_000, transcendentals=0)


def parts_of(x, count):
    parts = []
    for _ in range(count):
        parts.append(x.astype(BF16))
        x = x - parts[-1].astype(F32)
    return parts


def rotate(queries, rotation):
    high, low = parts_of(rotation, 2)
    return dot(queries, low) + dot(queries, high)


def ranks(owner, shards):
    rows, lanes = owner.shape
    tall = rows * shards
    spread = (iota((tall, rows), 0) // shards == iota((tall, rows), 1)).astype(BF16)
    hot = (dot(spread, owner.astype(BF16)) == (iota((tall, lanes), 0) % shards).astype(F32)).astype(BF16)
    before = (iota((lanes, lanes), 0) < iota((lanes, lanes), 1)).astype(BF16)
    r, c = iota((tall, tall), 0), iota((tall, tall), 1)
    earlier = ((r % shards == c % shards) & (c // shards < r // shards)).astype(BF16)
    count = dot(hot, before) + jnp.sum(dot(earlier, hot), axis=1, keepdims=True)
    return dot(spread, (hot.astype(F32) * count).astype(BF16), 0, 0).astype(I32)


def table_part(owner, rank, values, shards, kinds):
    rows, lanes = owner.shape
    line = iota((LANES, lanes), 0)
    kind, who = line // shards, line % shards
    left, right = [], []
    for c in range(rows):
        value = jnp.zeros((LANES, lanes), F32)
        for k, v in zip(kinds, values, strict=True):
            value = jnp.where(kind == k, v[c : c + 1], value)
        left.append(jnp.where(owner[c : c + 1] == who, value, 0.0))
        right.append((rank[c : c + 1] == line).astype(F32))
    total = jnp.zeros((LANES, LANES), F32)
    if lanes % LANES == 0:
        return dot(jnp.concatenate(left, 1).astype(BF16), jnp.concatenate(right, 1).astype(BF16), 1, 1)
    for l, r in zip(left, right, strict=True):
        total += dot(l.astype(BF16), r.astype(BF16), 1, 1)
    return total


def plan_kernel(shards, page_count, q_hbm, rot_hbm, probes_hbm, pages_hbm, rows_hbm, chunk_ref, probe_ref, place_ref, q_ref, held, probes_ref, pages_ref, rows_ref, sems):
    cands, rows = pages_ref.shape
    blocks, probes = probes_ref.shape
    pairs = [(pages_hbm, pages_ref), (rows_hbm, rows_ref), (probes_hbm, probes_ref), (q_hbm, q_ref)]
    pairs.append((rot_hbm.at[:, pl.ds(0, held.shape[1])], held))
    copies = [pltpu.make_async_copy(source, target, sems.at[i]) for i, (source, target) in enumerate(pairs)]
    for copy in copies:
        copy.start()
    for copy in copies[:3]:
        copy.wait()
    pages = pages_ref[...]
    owner = pages // page_count
    rank = ranks(owner, shards)
    place_ref[:cands] = owner
    place_ref[cands:] = rank
    query = iota((cands, rows), 1).astype(F32)
    values = (query, (pages % page_count).astype(F32), rows_ref[...].astype(F32))
    table = table_part(owner, rank, values, shards, (0, 1, 2))

    probe_pages = probes_ref[...]
    probe_owner = probe_pages // page_count
    probe_rank = ranks(probe_owner, shards)
    probe_ref[...] = probe_owner * (2 * blocks * probes // shards) + probe_rank
    value = (probe_pages % page_count + iota(probe_pages.shape, 0) * page_count).astype(F32)
    table += table_part(probe_owner, probe_rank, (value,), shards, (3,))
    table = table.astype(BF16)
    chunk_ref[rows:, :LANES] = table[: 2 * shards]
    chunk_ref[rows:, LANES : 2 * LANES] = table[2 * shards : 4 * shards]
    copies[3].wait()
    copies[4].wait()
    chunk_ref[:rows, :] = rotate(q_ref[...], held[...]).astype(BF16)


def tail_kernel(q_hbm, rot_hbm, tail_ref, q_ref, held, sems):
    count, _, width = held.shape
    copies = [pltpu.make_async_copy(q_hbm, q_ref, sems.at[count])]
    copies += [
        pltpu.make_async_copy(rot_hbm.at[:, pl.ds((i + 1) * width, width)], held.at[i], sems.at[i]) for i in range(count)
    ]
    for copy in copies:
        copy.start()
    copies[0].wait()
    for i in range(count):
        copies[1 + i].wait()
        tail_ref[:, i * width : (i + 1) * width] = rotate(q_ref[...], held[i]).astype(BF16)


def stack_kernel(*refs):
    out_ref = refs[-1]
    for i in range(out_ref.shape[0]):
        out_ref[i] = refs[i][...]


def relay_kernel(*refs):
    del refs


def coarse_kernel(shards, order, block_rows, me_ref, pieces, codes, *refs):
    score_ref, list_ref, lists, slots, slot_ref, sems = refs[-6:]
    capacity = score_ref.shape[1]
    page_count, page_rows, _ = codes.shape
    me = me_ref[0]
    rows = pieces.shape[1] - 2 * shards
    mine = iota((shards, 1), 0) == me
    for p in range(len(order)):
        first = jnp.sum(jnp.where(mine, pieces[p, rows : rows + shards, :].astype(F32), 0.0), axis=0, keepdims=True).astype(I32)
        second = jnp.sum(jnp.where(mine, pieces[p, rows + shards :, :].astype(F32), 0.0), axis=0, keepdims=True).astype(I32)
        lists[0, p : p + 1, :] = second[:, :LANES] * page_rows + first[:, LANES : 2 * LANES]
        lists[1, p : p + 1, :] = first[:, :LANES]
        slots[p : p + 1, :] = second[:, LANES : 2 * LANES]
    copy = pltpu.make_async_copy(slots, slot_ref, sems.at[0])
    copy.start()
    save = pltpu.make_async_copy(lists, list_ref, sems.at[1])
    save.start()
    copy.wait()
    for p, piece in enumerate(order):
        source = me ^ piece
        for s in range(capacity):
            slot = slot_ref[p, s]
            start = pl.multiple_of(slot // page_count * block_rows, block_rows)
            score_ref[source, s] = dot(pieces[p, pl.ds(start, block_rows), :], codes[slot % page_count], 1, 1).astype(BF16)
    save.wait()


def gather_kernel(list_a, list_b, lines_hbm, out_ref, index_ref, lines, sems):
    _, half, capacity, width = out_ref.shape
    count = sems.shape[0] - 2
    size = lines.shape[0] // count
    loads = [
        pltpu.make_async_copy(lines_hbm.at[pl.ds(i * size, size)], lines.at[pl.ds(i * size, size)], sems.at[i])
        for i in range(count)
    ]
    loads.append(pltpu.make_async_copy(list_a.at[0], index_ref.at[pl.ds(0, half)], sems.at[count]))
    loads.append(pltpu.make_async_copy(list_b.at[0], index_ref.at[pl.ds(half, half)], sems.at[count + 1]))
    for load in loads:
        load.start()
    for load in loads:
        load.wait()
    sublane = iota((8, width), 0)

    @pl.loop(0, 2 * half)
    def _(m):
        for g in range(0, capacity, 16):
            halves = []
            for h in range(g, g + 16, 8):
                eight = jnp.zeros((8, width), F32)
                for j in range(8):
                    row = jnp.broadcast_to(lines[pl.ds(index_ref[m, h + j], 1), :], (8, width))
                    eight = jnp.where(sublane == j, row, eight)
                halves.append(eight)
            out_ref[m // half, m % half, g : g + 16, :] = jnp.concatenate(halves, axis=0).astype(BF16)


def rerank_kernel(part, order, list_ref, rows_ref, heads, *refs):
    tails, before = refs[0], refs[1:-3]
    out_ref, query_ref, sem = refs[-3:]
    capacity = rows_ref.shape[2]
    queries = tails.shape[1]
    split = heads.shape[2]
    copy = pltpu.make_async_copy(list_ref.at[1], query_ref, sem)
    copy.start()
    if before:
        out_ref[...] = before[0][...]
    copy.wait()
    for p, m in enumerate(order):
        score = dot(heads[p, :queries, :], rows_ref[part, p, :, :split], 1, 1)
        score += dot(tails[p], rows_ref[part, p, :, split:], 1, 1)
        picked = iota(score.shape, 0) == query_ref[p : p + 1, :capacity]
        out_ref[m // 4, m % 4 : m % 4 + 1, :] = jnp.sum(jnp.where(picked, score, 0.0), axis=0, keepdims=True)


def pick_kernel(shards, me_ref, own_ref, y_ref, core_ref, both_ref, place_ref, placed_ref, out_ref, got):
    del placed_ref
    cands, rows = out_ref.shape
    capacity = got.shape[1]
    for a in range(shards // 4):
        for low, ref in enumerate((own_ref, core_ref, y_ref, both_ref)):
            got[4 * a + low : 4 * a + low + 1, :] = ref[a, low : low + 1, :]
    piece, rank = place_ref[:cands] ^ me_ref[0], place_ref[cands:]
    hot = [(piece[c : c + 1] == iota((shards, rows), 0)).astype(F32) for c in range(cands)]
    hot = jnp.concatenate(hot, axis=1).astype(BF16)
    high, middle, low = parts_of(got[...], 3)
    lines = dot(low, hot, 0, 0) + dot(middle, hot, 0, 0) + dot(high, hot, 0, 0)
    for c in range(cands):
        here = rank[c : c + 1] == iota((capacity, rows), 0)
        out_ref[c : c + 1, :] = jnp.sum(jnp.where(here, lines[:, c * rows : (c + 1) * rows], 0.0), axis=0, keepdims=True)


def place_kernel(place_ref, got_ref, out_ref, done_ref):
    blocks, probes = place_ref.shape
    _, block_rows, page_rows = got_ref.shape
    for b in range(blocks):
        for p in range(probes):
            out_ref[b * block_rows : (b + 1) * block_rows, p * page_rows : (p + 1) * page_rows] = got_ref[place_ref[b, p]]
    done_ref[...] = jnp.zeros_like(done_ref)


def exchange(x, mask, shards):
    return lax.ppermute(x, "idx", [(i, i ^ mask) for i in range(shards)])


def body(queries, rotation, codes, vectors, probes, cand_pages, cand_rows):
    shards = lax.axis_size("idx")
    me = lax.axis_index("idx").astype(I32).reshape(1)
    query_rows, full_width = queries.shape
    page_count, page_rows, proj_width = codes.shape
    block_count, probe_count = probes.shape
    block_rows = query_rows // block_count
    cand_count = cand_pages.shape[1]
    slot_count = block_count * probe_count
    capacity = 2 * slot_count // shards
    row_capacity = 2 * query_rows * cand_count // shards
    rest = full_width - proj_width
    assert proj_width == 2 * LANES and rest % proj_width == 0 and row_capacity <= LANES
    assert 4 * shards <= LANES and block_count * page_count <= 256 and query_rows <= 256 and page_rows <= 256

    chunk_rows = query_rows + 2 * shards
    chunk, probe_place, cand_place = pl.pallas_call(
        functools.partial(plan_kernel, shards, page_count),
        in_specs=[whole(HBM)] * 5,
        out_specs=[whole(VMEM)] * 3,
        out_shape=[
            jax.ShapeDtypeStruct((chunk_rows, proj_width), BF16),
            jax.ShapeDtypeStruct((block_count, probe_count), I32),
            jax.ShapeDtypeStruct((2 * cand_count, query_rows), I32),
        ],
        scratch_shapes=[
            pltpu.VMEM(queries.shape, BF16),
            pltpu.VMEM((full_width, proj_width), F32),
            pltpu.VMEM(probes.shape, I32),
            pltpu.VMEM((cand_count, query_rows), I32),
            pltpu.VMEM((cand_count, query_rows), I32),
            pltpu.SemaphoreType.DMA((5,)),
        ],
        compiler_params=params(61 * MIB),
        cost_estimate=cost(2),
        name="plan",
    )(queries, rotation, probes, cand_pages.T, cand_rows.T)
    tail = pl.pallas_call(
        tail_kernel,
        in_specs=[whole(ANY)] * 2,
        out_specs=whole(VMEM),
        out_shape=jax.ShapeDtypeStruct((query_rows, rest), BF16),
        scratch_shapes=[
            pltpu.VMEM(queries.shape, BF16),
            pltpu.VMEM((rest // proj_width, full_width, proj_width), F32),
            pltpu.SemaphoreType.DMA((rest // proj_width + 1,)),
        ],
        compiler_params=params(TAIL_MIB * MIB),
        cost_estimate=cost(3),
        name="rotate_tail",
    )(queries, rotation)

    masks = tuple(range(0, shards, 4))
    order = masks + tuple(m ^ 2 for m in masks)
    other = tuple(m ^ 1 for m in order)
    flat = vectors.reshape(page_count * page_rows, full_width)

    def stack(parts, waits, name):
        return pl.pallas_call(
            stack_kernel,
            in_specs=[whole(VMEM)] * len(parts) + [whole(ANY)] * len(waits),
            out_specs=whole(VMEM),
            out_shape=jax.ShapeDtypeStruct((len(parts), *parts[0].shape), BF16),
            compiler_params=params(10 * MIB),
            cost_estimate=cost(1),
            name=name,
        )(*parts, *waits)

    def relay(x, *waits):
        return pl.pallas_call(
            relay_kernel,
            in_specs=[whole(ANY)] * (1 + len(waits)),
            out_specs=whole(ANY),
            out_shape=jax.ShapeDtypeStruct(x.shape, x.dtype),
            input_output_aliases={0: 0},
            compiler_params=params(4 * MIB),
            cost_estimate=cost(1),
            name="relay",
        )(x, *waits)

    def coarse_scores(order, pieces, waits, before):
        count = 3 + len(waits)
        return pl.pallas_call(
            functools.partial(coarse_kernel, shards, order, block_rows),
            in_specs=[whole(SMEM), whole(VMEM), whole(VMEM)] + [whole(ANY)] * len(waits) + [whole(VMEM)] * len(before),
            out_specs=[whole(VMEM), whole(ANY)],
            out_shape=[
                jax.ShapeDtypeStruct((shards, capacity, block_rows, page_rows), BF16),
                jax.ShapeDtypeStruct((2, len(order), LANES), I32),
            ],
            scratch_shapes=[
                pltpu.VMEM((2, len(order), LANES), I32),
                pltpu.VMEM((len(order), LANES), I32),
                pltpu.SMEM((len(order), LANES), I32),
                pltpu.SemaphoreType.DMA((2,)),
            ],
            input_output_aliases={count: 0} if before else {},
            compiler_params=params(10 * MIB),
            cost_estimate=cost(COARSE_COST),
            name="coarse_scores",
        )(me, pieces, codes, *waits, *before)

    heads = [exchange(chunk, m, shards) if m else chunk for m in masks]
    heads += [exchange(x, 2, shards) for x in heads]
    tail = relay(tail, *heads[1 : len(masks)])
    tails = [exchange(tail, m, shards) if m else tail for m in masks]
    heads_a = stack(heads, tails[1:], "stack_heads")
    heads_b = exchange(heads_a, 1, shards)
    tails += [exchange(x, 2, shards) for x in tails]
    scored, list_a = coarse_scores(order, heads_a, [], [])
    scored, list_b = coarse_scores(other, heads_b, [], [scored])
    returned = lax.all_to_all(scored, "idx", split_axis=0, concat_axis=0, tiled=True)

    found = pl.pallas_call(
        gather_kernel,
        in_specs=[whole(ANY)] * 3,
        out_specs=whole(VMEM),
        out_shape=jax.ShapeDtypeStruct((2, len(order), row_capacity, full_width), BF16),
        scratch_shapes=[
            pltpu.SMEM((shards, LANES), I32),
            pltpu.VMEM(flat.shape, F32),
            pltpu.SemaphoreType.DMA((6,)),
        ],
        compiler_params=params(34 * MIB),
        cost_estimate=cost(GATHER_COST),
        name="gather_rows",
    )(list_a, list_b, flat)
    tails_a = stack(tails, [found], "stack_tails")
    tails_b = exchange(tails_a, 1, shards)

    def scores(part, order, list_ref, heads, tails, before):
        return pl.pallas_call(
            functools.partial(rerank_kernel, part, order),
            in_specs=[whole(ANY)] + [whole(VMEM)] * (3 + len(before)),
            out_specs=whole(VMEM),
            out_shape=jax.ShapeDtypeStruct((shards // 4, 4, row_capacity), F32),
            scratch_shapes=[pltpu.VMEM((len(order), LANES), I32), pltpu.SemaphoreType.DMA],
            compiler_params=params(10 * MIB),
            cost_estimate=cost(RERANK_COST),
            name="rerank_scores",
        )(list_ref, found, heads, tails, *before)

    answers = scores(0, order, list_a, heads_a, tails_a, [])
    answers = scores(1, other, list_b, heads_b, tails_b, [answers])
    own = jnp.stack([exchange(answers[a], 4 * a, shards) if a else answers[a] for a in range(shards // 4)])
    across = exchange(own, 2, shards)
    coarse, placed = pl.pallas_call(
        place_kernel,
        in_specs=[whole(SMEM), whole(VMEM)],
        out_specs=[whole(VMEM)] * 2,
        out_shape=[
            jax.ShapeDtypeStruct((query_rows, probe_count * page_rows), BF16),
            jax.ShapeDtypeStruct((8, LANES), F32),
        ],
        compiler_params=params(10 * MIB),
        cost_estimate=cost(1),
        name="place_scores",
    )(probe_place, returned.reshape(shards * capacity, block_rows, page_rows))
    rerank = pl.pallas_call(
        functools.partial(pick_kernel, shards),
        in_specs=[whole(SMEM)] + [whole(VMEM)] * 6,
        out_specs=whole(VMEM),
        out_shape=jax.ShapeDtypeStruct((cand_count, query_rows), F32),
        scratch_shapes=[pltpu.VMEM((shards, row_capacity), F32)],
        compiler_params=params(10 * MIB),
        cost_estimate=cost(1),
        name="pick_answers",
    )(me, own, across, exchange(own, 1, shards), exchange(own, 3, shards), cand_place, placed).T
    return coarse, rerank


def solution(mesh):
    split = P(("grp", "idx"))
    in_specs = (split, P(), split, split, split, split, split)
    return jax.shard_map(body, mesh=mesh, in_specs=in_specs, out_specs=(split, split), check_vma=False)
```

```python
import functools

import jax
import jax.numpy as jnp
from jax import lax
from jax.experimental import pallas as pl
from jax.experimental.pallas import tpu as pltpu
from jax.sharding import PartitionSpec as P

LANES = 128
MIB = 1 << 20
TAIL_MIB = 58
COARSE_COST, GATHER_COST, RERANK_COST = 3, 12, 1
F32, BF16, I32 = jnp.float32, jnp.bfloat16, jnp.int32
VMEM, SMEM, HBM, ANY = pltpu.VMEM, pltpu.SMEM, pltpu.HBM, pl.ANY


def iota(shape, axis):
    return lax.broadcasted_iota(I32, shape, axis)


def dot(a, b, over_a=1, over_b=0):
    return lax.dot_general(a, b, (((over_a,), (over_b,)), ((), ())), preferred_element_type=F32)


def params(limit, **more):
    return pltpu.CompilerParams(vmem_limit_bytes=limit, **more)


def whole(space):
    return pl.BlockSpec(memory_space=space)


def cost(us):
    return pl.CostEstimate(flops=0, bytes_accessed=us * 3_000_000, transcendentals=0)


def parts_of(x, count):
    parts = []
    for _ in range(count):
        parts.append(x.astype(BF16))
        x = x - parts[-1].astype(F32)
    return parts


def rotate(queries, rotation):
    high, low = parts_of(rotation, 2)
    return dot(queries, low) + dot(queries, high)


def ranks(owner, shards):
    rows, lanes = owner.shape
    tall = rows * shards
    spread = (iota((tall, rows), 0) // shards == iota((tall, rows), 1)).astype(BF16)
    hot = (dot(spread, owner.astype(BF16)) == (iota((tall, lanes), 0) % shards).astype(F32)).astype(BF16)
    before = (iota((lanes, lanes), 0) < iota((lanes, lanes), 1)).astype(BF16)
    r, c = iota((tall, tall), 0), iota((tall, tall), 1)
    earlier = ((r % shards == c % shards) & (c // shards < r // shards)).astype(BF16)
    count = dot(hot, before) + jnp.sum(dot(earlier, hot), axis=1, keepdims=True)
    return dot(spread, (hot.astype(F32) * count).astype(BF16), 0, 0).astype(I32)


def table_part(owner, rank, values, shards, kinds):
    rows, lanes = owner.shape
    line = iota((LANES, lanes), 0)
    kind, who = line // shards, line % shards
    left, right = [], []
    for c in range(rows):
        value = jnp.zeros((LANES, lanes), F32)
        for k, v in zip(kinds, values, strict=True):
            value = jnp.where(kind == k, v[c : c + 1], value)
        left.append(jnp.where(owner[c : c + 1] == who, value, 0.0))
        right.append((rank[c : c + 1] == line).astype(F32))
    total = jnp.zeros((LANES, LANES), F32)
    if lanes % LANES == 0:
        return dot(jnp.concatenate(left, 1).astype(BF16), jnp.concatenate(right, 1).astype(BF16), 1, 1)
    for l, r in zip(left, right, strict=True):
        total += dot(l.astype(BF16), r.astype(BF16), 1, 1)
    return total


def plan_kernel(shards, page_count, q_hbm, rot_hbm, probes_hbm, pages_hbm, rows_hbm, chunk_ref, probe_ref, place_ref, q_ref, held, probes_ref, pages_ref, rows_ref, sems):
    cands, rows = pages_ref.shape
    blocks, probes = probes_ref.shape
    pairs = [(pages_hbm, pages_ref), (rows_hbm, rows_ref), (probes_hbm, probes_ref), (q_hbm, q_ref)]
    pairs.append((rot_hbm.at[:, pl.ds(0, held.shape[1])], held))
    copies = [pltpu.make_async_copy(source, target, sems.at[i]) for i, (source, target) in enumerate(pairs)]
    for copy in copies:
        copy.start()
    for copy in copies[:3]:
        copy.wait()
    pages = pages_ref[...]
    owner = pages // page_count
    rank = ranks(owner, shards)
    place_ref[:cands] = owner
    place_ref[cands:] = rank
    query = iota((cands, rows), 1).astype(F32)
    values = (query, (pages % page_count).astype(F32), rows_ref[...].astype(F32))
    table = table_part(owner, rank, values, shards, (0, 1, 2))

    probe_pages = probes_ref[...]
    probe_owner = probe_pages // page_count
    probe_rank = ranks(probe_owner, shards)
    probe_ref[...] = probe_owner * (2 * blocks * probes // shards) + probe_rank
    value = (probe_pages % page_count + iota(probe_pages.shape, 0) * page_count).astype(F32)
    table += table_part(probe_owner, probe_rank, (value,), shards, (3,))
    table = table.astype(BF16)
    chunk_ref[rows:, :LANES] = table[: 2 * shards]
    chunk_ref[rows:, LANES : 2 * LANES] = table[2 * shards : 4 * shards]
    copies[3].wait()
    copies[4].wait()
    chunk_ref[:rows, :] = rotate(q_ref[...], held[...]).astype(BF16)


def tail_kernel(q_hbm, rot_hbm, tail_ref, q_ref, held, sems):
    count, _, width = held.shape
    copies = [pltpu.make_async_copy(q_hbm, q_ref, sems.at[count])]
    copies += [
        pltpu.make_async_copy(rot_hbm.at[:, pl.ds((i + 1) * width, width)], held.at[i], sems.at[i]) for i in range(count)
    ]
    for copy in copies:
        copy.start()
    copies[0].wait()
    for i in range(count):
        copies[1 + i].wait()
        tail_ref[:, i * width : (i + 1) * width] = rotate(q_ref[...], held[i]).astype(BF16)


def stack_kernel(*refs):
    out_ref = refs[-1]
    for i in range(out_ref.shape[0]):
        out_ref[i] = refs[i][...]


def relay_kernel(*refs):
    del refs


def coarse_kernel(shards, order, block_rows, me_ref, pieces, codes, *refs):
    score_ref, list_ref, lists, slots, slot_ref, sems = refs[-6:]
    capacity = score_ref.shape[1]
    page_count, page_rows, _ = codes.shape
    me = me_ref[0]
    rows = pieces.shape[1] - 2 * shards
    mine = iota((shards, 1), 0) == me
    for p in range(len(order)):
        first = jnp.sum(jnp.where(mine, pieces[p, rows : rows + shards, :].astype(F32), 0.0), axis=0, keepdims=True).astype(I32)
        second = jnp.sum(jnp.where(mine, pieces[p, rows + shards :, :].astype(F32), 0.0), axis=0, keepdims=True).astype(I32)
        lists[0, p : p + 1, :] = second[:, :LANES] * page_rows + first[:, LANES : 2 * LANES]
        lists[1, p : p + 1, :] = first[:, :LANES]
        slots[p : p + 1, :] = second[:, LANES : 2 * LANES]
    copy = pltpu.make_async_copy(slots, slot_ref, sems.at[0])
    copy.start()
    save = pltpu.make_async_copy(lists, list_ref, sems.at[1])
    save.start()
    copy.wait()
    for p, piece in enumerate(order):
        source = me ^ piece
        for s in range(capacity):
            slot = slot_ref[p, s]
            start = pl.multiple_of(slot // page_count * block_rows, block_rows)
            score_ref[source, s] = dot(pieces[p, pl.ds(start, block_rows), :], codes[slot % page_count], 1, 1).astype(BF16)
    save.wait()


def gather_kernel(list_a, list_b, lines_hbm, out_ref, index_ref, lines, sems):
    _, half, capacity, width = out_ref.shape
    count = sems.shape[0] - 2
    size = lines.shape[0] // count
    loads = [
        pltpu.make_async_copy(lines_hbm.at[pl.ds(i * size, size)], lines.at[pl.ds(i * size, size)], sems.at[i])
        for i in range(count)
    ]
    loads.append(pltpu.make_async_copy(list_a.at[0], index_ref.at[pl.ds(0, half)], sems.at[count]))
    loads.append(pltpu.make_async_copy(list_b.at[0], index_ref.at[pl.ds(half, half)], sems.at[count + 1]))
    for load in loads:
        load.start()
    for load in loads:
        load.wait()
    sublane = iota((8, width), 0)

    @pl.loop(0, 2 * half)
    def _(m):
        for g in range(0, capacity, 16):
            halves = []
            for h in range(g, g + 16, 8):
                eight = jnp.zeros((8, width), F32)
                for j in range(8):
                    row = jnp.broadcast_to(lines[pl.ds(index_ref[m, h + j], 1), :], (8, width))
                    eight = jnp.where(sublane == j, row, eight)
                halves.append(eight)
            out_ref[m // half, m % half, g : g + 16, :] = jnp.concatenate(halves, axis=0).astype(BF16)


def rerank_kernel(part, order, list_ref, rows_ref, heads, *refs):
    tails, before = refs[0], refs[1:-3]
    out_ref, query_ref, sem = refs[-3:]
    capacity = rows_ref.shape[2]
    queries = tails.shape[1]
    split = heads.shape[2]
    copy = pltpu.make_async_copy(list_ref.at[1], query_ref, sem)
    copy.start()
    if before:
        out_ref[...] = before[0][...]
    copy.wait()
    for p, m in enumerate(order):
        score = dot(heads[p, :queries, :], rows_ref[part, p, :, :split], 1, 1)
        score += dot(tails[p], rows_ref[part, p, :, split:], 1, 1)
        picked = iota(score.shape, 0) == query_ref[p : p + 1, :capacity]
        out_ref[m // 4, m % 4 : m % 4 + 1, :] = jnp.sum(jnp.where(picked, score, 0.0), axis=0, keepdims=True)


def pick_kernel(shards, me_ref, own_ref, y_ref, core_ref, both_ref, place_ref, placed_ref, out_ref, got):
    del placed_ref
    cands, rows = out_ref.shape
    capacity = got.shape[1]
    for a in range(shards // 4):
        for low, ref in enumerate((own_ref, core_ref, y_ref, both_ref)):
            got[4 * a + low : 4 * a + low + 1, :] = ref[a, low : low + 1, :]
    piece, rank = place_ref[:cands] ^ me_ref[0], place_ref[cands:]
    hot = [(piece[c : c + 1] == iota((shards, rows), 0)).astype(F32) for c in range(cands)]
    hot = jnp.concatenate(hot, axis=1).astype(BF16)
    high, middle, low = parts_of(got[...], 3)
    lines = dot(low, hot, 0, 0) + dot(middle, hot, 0, 0) + dot(high, hot, 0, 0)
    for c in range(cands):
        here = rank[c : c + 1] == iota((capacity, rows), 0)
        out_ref[c : c + 1, :] = jnp.sum(jnp.where(here, lines[:, c * rows : (c + 1) * rows], 0.0), axis=0, keepdims=True)


def place_kernel(place_ref, got_ref, out_ref, done_ref):
    blocks, probes = place_ref.shape
    _, block_rows, page_rows = got_ref.shape
    for b in range(blocks):
        for p in range(probes):
            out_ref[b * block_rows : (b + 1) * block_rows, p * page_rows : (p + 1) * page_rows] = got_ref[place_ref[b, p]]
    done_ref[...] = jnp.zeros_like(done_ref)


def exchange(x, mask, shards):
    return lax.ppermute(x, "idx", [(i, i ^ mask) for i in range(shards)])


def body(queries, rotation, codes, vectors, probes, cand_pages, cand_rows):
    shards = lax.axis_size("idx")
    me = lax.axis_index("idx").astype(I32).reshape(1)
    query_rows, full_width = queries.shape
    page_count, page_rows, proj_width = codes.shape
    block_count, probe_count = probes.shape
    block_rows = query_rows // block_count
    cand_count = cand_pages.shape[1]
    slot_count = block_count * probe_count
    capacity = 2 * slot_count // shards
    row_capacity = 2 * query_rows * cand_count // shards
    rest = full_width - proj_width
    assert proj_width == 2 * LANES and rest % proj_width == 0 and row_capacity <= LANES
    assert 4 * shards <= LANES and block_count * page_count <= 256 and query_rows <= 256 and page_rows <= 256

    chunk_rows = query_rows + 2 * shards
    chunk, probe_place, cand_place = pl.pallas_call(
        functools.partial(plan_kernel, shards, page_count),
        in_specs=[whole(HBM)] * 5,
        out_specs=[whole(VMEM)] * 3,
        out_shape=[
            jax.ShapeDtypeStruct((chunk_rows, proj_width), BF16),
            jax.ShapeDtypeStruct((block_count, probe_count), I32),
            jax.ShapeDtypeStruct((2 * cand_count, query_rows), I32),
        ],
        scratch_shapes=[
            pltpu.VMEM(queries.shape, BF16),
            pltpu.VMEM((full_width, proj_width), F32),
            pltpu.VMEM(probes.shape, I32),
            pltpu.VMEM((cand_count, query_rows), I32),
            pltpu.VMEM((cand_count, query_rows), I32),
            pltpu.SemaphoreType.DMA((5,)),
        ],
        compiler_params=params(61 * MIB),
        cost_estimate=cost(2),
        name="plan",
    )(queries, rotation, probes, cand_pages.T, cand_rows.T)
    tail = pl.pallas_call(
        tail_kernel,
        in_specs=[whole(ANY)] * 2,
        out_specs=whole(VMEM),
        out_shape=jax.ShapeDtypeStruct((query_rows, rest), BF16),
        scratch_shapes=[
            pltpu.VMEM(queries.shape, BF16),
            pltpu.VMEM((rest // proj_width, full_width, proj_width), F32),
            pltpu.SemaphoreType.DMA((rest // proj_width + 1,)),
        ],
        compiler_params=params(TAIL_MIB * MIB),
        cost_estimate=cost(3),
        name="rotate_tail",
    )(queries, rotation)

    masks = tuple(range(0, shards, 4))
    order = masks + tuple(m ^ 2 for m in masks)
    other = tuple(m ^ 1 for m in order)
    flat = vectors.reshape(page_count * page_rows, full_width)

    def stack(parts, waits, name):
        return pl.pallas_call(
            stack_kernel,
            in_specs=[whole(VMEM)] * len(parts) + [whole(ANY)] * len(waits),
            out_specs=whole(VMEM),
            out_shape=jax.ShapeDtypeStruct((len(parts), *parts[0].shape), BF16),
            compiler_params=params(10 * MIB),
            cost_estimate=cost(1),
            name=name,
        )(*parts, *waits)

    def relay(x, *waits):
        return pl.pallas_call(
            relay_kernel,
            in_specs=[whole(ANY)] * (1 + len(waits)),
            out_specs=whole(ANY),
            out_shape=jax.ShapeDtypeStruct(x.shape, x.dtype),
            input_output_aliases={0: 0},
            compiler_params=params(4 * MIB),
            cost_estimate=cost(1),
            name="relay",
        )(x, *waits)

    def coarse_scores(order, pieces, waits, before):
        count = 3 + len(waits)
        return pl.pallas_call(
            functools.partial(coarse_kernel, shards, order, block_rows),
            in_specs=[whole(SMEM), whole(VMEM), whole(VMEM)] + [whole(ANY)] * len(waits) + [whole(VMEM)] * len(before),
            out_specs=[whole(VMEM), whole(ANY)],
            out_shape=[
                jax.ShapeDtypeStruct((shards, capacity, block_rows, page_rows), BF16),
                jax.ShapeDtypeStruct((2, len(order), LANES), I32),
            ],
            scratch_shapes=[
                pltpu.VMEM((2, len(order), LANES), I32),
                pltpu.VMEM((len(order), LANES), I32),
                pltpu.SMEM((len(order), LANES), I32),
                pltpu.SemaphoreType.DMA((2,)),
            ],
            input_output_aliases={count: 0} if before else {},
            compiler_params=params(10 * MIB),
            cost_estimate=cost(COARSE_COST),
            name="coarse_scores",
        )(me, pieces, codes, *waits, *before)

    heads = [exchange(chunk, m, shards) if m else chunk for m in masks]
    heads += [exchange(x, 2, shards) for x in heads]
    tail = relay(tail, heads[1], heads[2])
    tails = [exchange(tail, m, shards) if m else tail for m in masks]
    heads_a = stack(heads, tails[1:], "stack_heads")
    heads_b = exchange(heads_a, 1, shards)
    tails += [exchange(x, 2, shards) for x in tails]
    scored, list_a = coarse_scores(order, heads_a, [], [])
    scored, list_b = coarse_scores(other, heads_b, [], [scored])
    returned = lax.all_to_all(scored, "idx", split_axis=0, concat_axis=0, tiled=True)

    found = pl.pallas_call(
        gather_kernel,
        in_specs=[whole(ANY)] * 3,
        out_specs=whole(VMEM),
        out_shape=jax.ShapeDtypeStruct((2, len(order), row_capacity, full_width), BF16),
        scratch_shapes=[
            pltpu.SMEM((shards, LANES), I32),
            pltpu.VMEM(flat.shape, F32),
            pltpu.SemaphoreType.DMA((6,)),
        ],
        compiler_params=params(34 * MIB),
        cost_estimate=cost(GATHER_COST),
        name="gather_rows",
    )(list_a, list_b, flat)
    tails_a = stack(tails, [found], "stack_tails")
    tails_b = exchange(tails_a, 1, shards)

    def scores(part, order, list_ref, heads, tails, before):
        return pl.pallas_call(
            functools.partial(rerank_kernel, part, order),
            in_specs=[whole(ANY)] + [whole(VMEM)] * (3 + len(before)),
            out_specs=whole(VMEM),
            out_shape=jax.ShapeDtypeStruct((shards // 4, 4, row_capacity), F32),
            scratch_shapes=[pltpu.VMEM((len(order), LANES), I32), pltpu.SemaphoreType.DMA],
            compiler_params=params(10 * MIB),
            cost_estimate=cost(RERANK_COST),
            name="rerank_scores",
        )(list_ref, found, heads, tails, *before)

    answers = scores(0, order, list_a, heads_a, tails_a, [])
    answers = scores(1, other, list_b, heads_b, tails_b, [answers])
    own = jnp.stack([exchange(answers[a], 4 * a, shards) if a else answers[a] for a in range(shards // 4)])
    across = exchange(own, 2, shards)
    coarse, placed = pl.pallas_call(
        place_kernel,
        in_specs=[whole(SMEM), whole(VMEM)],
        out_specs=[whole(VMEM)] * 2,
        out_shape=[
            jax.ShapeDtypeStruct((query_rows, probe_count * page_rows), BF16),
            jax.ShapeDtypeStruct((8, LANES), F32),
        ],
        compiler_params=params(10 * MIB),
        cost_estimate=cost(1),
        name="place_scores",
    )(probe_place, returned.reshape(shards * capacity, block_rows, page_rows))
    rerank = pl.pallas_call(
        functools.partial(pick_kernel, shards),
        in_specs=[whole(SMEM)] + [whole(VMEM)] * 6,
        out_specs=whole(VMEM),
        out_shape=jax.ShapeDtypeStruct((cand_count, query_rows), F32),
        scratch_shapes=[pltpu.VMEM((shards, row_capacity), F32)],
        compiler_params=params(10 * MIB),
        cost_estimate=cost(1),
        name="pick_answers",
    )(me, own, across, exchange(own, 1, shards), exchange(own, 3, shards), cand_place, placed).T
    return coarse, rerank


def solution(mesh):
    split = P(("grp", "idx"))
    in_specs = (split, P(), split, split, split, split, split)
    return jax.shard_map(body, mesh=mesh, in_specs=in_specs, out_specs=(split, split), check_vma=False)
```

```python
import functools

import jax
import jax.numpy as jnp
from jax import lax
from jax.experimental import pallas as pl
from jax.experimental.pallas import tpu as pltpu
from jax.sharding import PartitionSpec as P

LANES = 128
MIB = 1 << 20
TAIL_MIB = 58
COARSE_COST, GATHER_COST, RERANK_COST = 3, 12, 1
F32, BF16, I32 = jnp.float32, jnp.bfloat16, jnp.int32
VMEM, SMEM, HBM, ANY = pltpu.VMEM, pltpu.SMEM, pltpu.HBM, pl.ANY


def iota(shape, axis):
    return lax.broadcasted_iota(I32, shape, axis)


def dot(a, b, over_a=1, over_b=0):
    return lax.dot_general(a, b, (((over_a,), (over_b,)), ((), ())), preferred_element_type=F32)


def params(limit, **more):
    return pltpu.CompilerParams(vmem_limit_bytes=limit, **more)


def whole(space):
    return pl.BlockSpec(memory_space=space)


def cost(us):
    return pl.CostEstimate(flops=0, bytes_accessed=us * 3_000_000, transcendentals=0)


def parts_of(x, count):
    parts = []
    for _ in range(count):
        parts.append(x.astype(BF16))
        x = x - parts[-1].astype(F32)
    return parts


def rotate(queries, rotation):
    high, low = parts_of(rotation, 2)
    return dot(queries, low) + dot(queries, high)


def ranks(owner, shards):
    rows, lanes = owner.shape
    tall = rows * shards
    spread = (iota((tall, rows), 0) // shards == iota((tall, rows), 1)).astype(BF16)
    hot = (dot(spread, owner.astype(BF16)) == (iota((tall, lanes), 0) % shards).astype(F32)).astype(BF16)
    before = (iota((lanes, lanes), 0) < iota((lanes, lanes), 1)).astype(BF16)
    r, c = iota((tall, tall), 0), iota((tall, tall), 1)
    earlier = ((r % shards == c % shards) & (c // shards < r // shards)).astype(BF16)
    count = dot(hot, before) + jnp.sum(dot(earlier, hot), axis=1, keepdims=True)
    return dot(spread, (hot.astype(F32) * count).astype(BF16), 0, 0).astype(I32)


def table_part(owner, rank, values, shards, kinds):
    rows, lanes = owner.shape
    line = iota((LANES, lanes), 0)
    kind, who = line // shards, line % shards
    left, right = [], []
    for c in range(rows):
        value = jnp.zeros((LANES, lanes), F32)
        for k, v in zip(kinds, values, strict=True):
            value = jnp.where(kind == k, v[c : c + 1], value)
        left.append(jnp.where(owner[c : c + 1] == who, value, 0.0))
        right.append((rank[c : c + 1] == line).astype(F32))
    total = jnp.zeros((LANES, LANES), F32)
    if lanes % LANES == 0:
        return dot(jnp.concatenate(left, 1).astype(BF16), jnp.concatenate(right, 1).astype(BF16), 1, 1)
    for l, r in zip(left, right, strict=True):
        total += dot(l.astype(BF16), r.astype(BF16), 1, 1)
    return total


def plan_kernel(shards, page_count, q_hbm, rot_hbm, probes_hbm, pages_hbm, rows_hbm, chunk_ref, probe_ref, place_ref, q_ref, held, probes_ref, pages_ref, rows_ref, sems):
    cands, rows = pages_ref.shape
    blocks, probes = probes_ref.shape
    pairs = [(pages_hbm, pages_ref), (rows_hbm, rows_ref), (probes_hbm, probes_ref), (q_hbm, q_ref)]
    pairs.append((rot_hbm.at[:, pl.ds(0, held.shape[1])], held))
    copies = [pltpu.make_async_copy(source, target, sems.at[i]) for i, (source, target) in enumerate(pairs)]
    for copy in copies:
        copy.start()
    for copy in copies[:3]:
        copy.wait()
    pages = pages_ref[...]
    owner = pages // page_count
    rank = ranks(owner, shards)
    place_ref[:cands] = owner
    place_ref[cands:] = rank
    query = iota((cands, rows), 1).astype(F32)
    values = (query, (pages % page_count).astype(F32), rows_ref[...].astype(F32))
    table = table_part(owner, rank, values, shards, (0, 1, 2))

    probe_pages = probes_ref[...]
    probe_owner = probe_pages // page_count
    probe_rank = ranks(probe_owner, shards)
    probe_ref[...] = probe_owner * (2 * blocks * probes // shards) + probe_rank
    value = (probe_pages % page_count + iota(probe_pages.shape, 0) * page_count).astype(F32)
    table += table_part(probe_owner, probe_rank, (value,), shards, (3,))
    table = table.astype(BF16)
    chunk_ref[rows:, :LANES] = table[: 2 * shards]
    chunk_ref[rows:, LANES : 2 * LANES] = table[2 * shards : 4 * shards]
    copies[3].wait()
    copies[4].wait()
    chunk_ref[:rows, :] = rotate(q_ref[...], held[...]).astype(BF16)


def tail_kernel(q_hbm, rot_hbm, tail_ref, q_ref, held, sems):
    count, _, width = held.shape
    copies = [pltpu.make_async_copy(q_hbm, q_ref, sems.at[count])]
    copies += [
        pltpu.make_async_copy(rot_hbm.at[:, pl.ds((i + 1) * width, width)], held.at[i], sems.at[i]) for i in range(count)
    ]
    for copy in copies:
        copy.start()
    copies[0].wait()
    for i in range(count):
        copies[1 + i].wait()
        tail_ref[:, i * width : (i + 1) * width] = rotate(q_ref[...], held[i]).astype(BF16)


def stack_kernel(*refs):
    out_ref = refs[-1]
    for i in range(out_ref.shape[0]):
        out_ref[i] = refs[i][...]


def relay_kernel(in_ref, *refs):
    refs[-1][...] = in_ref[...]


def coarse_kernel(shards, order, block_rows, me_ref, pieces, codes, *refs):
    score_ref, list_ref, lists, slots, slot_ref, sems = refs[-6:]
    capacity = score_ref.shape[1]
    page_count, page_rows, _ = codes.shape
    me = me_ref[0]
    rows = pieces.shape[1] - 2 * shards
    mine = iota((shards, 1), 0) == me
    for p in range(len(order)):
        first = jnp.sum(jnp.where(mine, pieces[p, rows : rows + shards, :].astype(F32), 0.0), axis=0, keepdims=True).astype(I32)
        second = jnp.sum(jnp.where(mine, pieces[p, rows + shards :, :].astype(F32), 0.0), axis=0, keepdims=True).astype(I32)
        lists[0, p : p + 1, :] = second[:, :LANES] * page_rows + first[:, LANES : 2 * LANES]
        lists[1, p : p + 1, :] = first[:, :LANES]
        slots[p : p + 1, :] = second[:, LANES : 2 * LANES]
    copy = pltpu.make_async_copy(slots, slot_ref, sems.at[0])
    copy.start()
    save = pltpu.make_async_copy(lists, list_ref, sems.at[1])
    save.start()
    copy.wait()
    for p, piece in enumerate(order):
        source = me ^ piece
        for s in range(capacity):
            slot = slot_ref[p, s]
            start = pl.multiple_of(slot // page_count * block_rows, block_rows)
            score_ref[source, s] = dot(pieces[p, pl.ds(start, block_rows), :], codes[slot % page_count], 1, 1).astype(BF16)
    save.wait()


def gather_kernel(list_a, list_b, lines_hbm, out_ref, index_ref, lines, sems):
    _, half, capacity, width = out_ref.shape
    count = sems.shape[0] - 2
    size = lines.shape[0] // count
    loads = [
        pltpu.make_async_copy(lines_hbm.at[pl.ds(i * size, size)], lines.at[pl.ds(i * size, size)], sems.at[i])
        for i in range(count)
    ]
    loads.append(pltpu.make_async_copy(list_a.at[0], index_ref.at[pl.ds(0, half)], sems.at[count]))
    loads.append(pltpu.make_async_copy(list_b.at[0], index_ref.at[pl.ds(half, half)], sems.at[count + 1]))
    for load in loads:
        load.start()
    for load in loads:
        load.wait()
    sublane = iota((8, width), 0)

    @pl.loop(0, 2 * half)
    def _(m):
        for g in range(0, capacity, 16):
            halves = []
            for h in range(g, g + 16, 8):
                eight = jnp.zeros((8, width), F32)
                for j in range(8):
                    row = jnp.broadcast_to(lines[pl.ds(index_ref[m, h + j], 1), :], (8, width))
                    eight = jnp.where(sublane == j, row, eight)
                halves.append(eight)
            out_ref[m // half, m % half, g : g + 16, :] = jnp.concatenate(halves, axis=0).astype(BF16)


def rerank_kernel(part, order, list_ref, rows_ref, heads, *refs):
    tails, before = refs[0], refs[1:-3]
    out_ref, query_ref, sem = refs[-3:]
    capacity = rows_ref.shape[2]
    queries = tails.shape[1]
    split = heads.shape[2]
    copy = pltpu.make_async_copy(list_ref.at[1], query_ref, sem)
    copy.start()
    if before:
        out_ref[...] = before[0][...]
    copy.wait()
    for p, m in enumerate(order):
        score = dot(heads[p, :queries, :], rows_ref[part, p, :, :split], 1, 1)
        score += dot(tails[p], rows_ref[part, p, :, split:], 1, 1)
        picked = iota(score.shape, 0) == query_ref[p : p + 1, :capacity]
        out_ref[m // 4, m % 4 : m % 4 + 1, :] = jnp.sum(jnp.where(picked, score, 0.0), axis=0, keepdims=True)


def pick_kernel(shards, me_ref, own_ref, y_ref, core_ref, both_ref, place_ref, placed_ref, out_ref, got):
    del placed_ref
    cands, rows = out_ref.shape
    capacity = got.shape[1]
    for a in range(shards // 4):
        for low, ref in enumerate((own_ref, core_ref, y_ref, both_ref)):
            got[4 * a + low : 4 * a + low + 1, :] = ref[a, low : low + 1, :]
    piece, rank = place_ref[:cands] ^ me_ref[0], place_ref[cands:]
    hot = [(piece[c : c + 1] == iota((shards, rows), 0)).astype(F32) for c in range(cands)]
    hot = jnp.concatenate(hot, axis=1).astype(BF16)
    high, middle, low = parts_of(got[...], 3)
    lines = dot(low, hot, 0, 0) + dot(middle, hot, 0, 0) + dot(high, hot, 0, 0)
    for c in range(cands):
        here = rank[c : c + 1] == iota((capacity, rows), 0)
        out_ref[c : c + 1, :] = jnp.sum(jnp.where(here, lines[:, c * rows : (c + 1) * rows], 0.0), axis=0, keepdims=True)


def place_kernel(place_ref, got_ref, out_ref, done_ref):
    blocks, probes = place_ref.shape
    _, block_rows, page_rows = got_ref.shape
    for b in range(blocks):
        for p in range(probes):
            out_ref[b * block_rows : (b + 1) * block_rows, p * page_rows : (p + 1) * page_rows] = got_ref[place_ref[b, p]]
    done_ref[...] = jnp.zeros_like(done_ref)


def exchange(x, mask, shards):
    return lax.ppermute(x, "idx", [(i, i ^ mask) for i in range(shards)])


def body(queries, rotation, codes, vectors, probes, cand_pages, cand_rows):
    shards = lax.axis_size("idx")
    me = lax.axis_index("idx").astype(I32).reshape(1)
    query_rows, full_width = queries.shape
    page_count, page_rows, proj_width = codes.shape
    block_count, probe_count = probes.shape
    block_rows = query_rows // block_count
    cand_count = cand_pages.shape[1]
    slot_count = block_count * probe_count
    capacity = 2 * slot_count // shards
    row_capacity = 2 * query_rows * cand_count // shards
    rest = full_width - proj_width
    assert proj_width == 2 * LANES and rest % proj_width == 0 and row_capacity <= LANES
    assert 4 * shards <= LANES and block_count * page_count <= 256 and query_rows <= 256 and page_rows <= 256

    chunk_rows = query_rows + 2 * shards
    chunk, probe_place, cand_place = pl.pallas_call(
        functools.partial(plan_kernel, shards, page_count),
        in_specs=[whole(HBM)] * 5,
        out_specs=[whole(VMEM)] * 3,
        out_shape=[
            jax.ShapeDtypeStruct((chunk_rows, proj_width), BF16),
            jax.ShapeDtypeStruct((block_count, probe_count), I32),
            jax.ShapeDtypeStruct((2 * cand_count, query_rows), I32),
        ],
        scratch_shapes=[
            pltpu.VMEM(queries.shape, BF16),
            pltpu.VMEM((full_width, proj_width), F32),
            pltpu.VMEM(probes.shape, I32),
            pltpu.VMEM((cand_count, query_rows), I32),
            pltpu.VMEM((cand_count, query_rows), I32),
            pltpu.SemaphoreType.DMA((5,)),
        ],
        compiler_params=params(61 * MIB),
        cost_estimate=cost(2),
        name="plan",
    )(queries, rotation, probes, cand_pages.T, cand_rows.T)
    tail = pl.pallas_call(
        tail_kernel,
        in_specs=[whole(ANY)] * 2,
        out_specs=whole(VMEM),
        out_shape=jax.ShapeDtypeStruct((query_rows, rest), BF16),
        scratch_shapes=[
            pltpu.VMEM(queries.shape, BF16),
            pltpu.VMEM((rest // proj_width, full_width, proj_width), F32),
            pltpu.SemaphoreType.DMA((rest // proj_width + 1,)),
        ],
        compiler_params=params(TAIL_MIB * MIB),
        cost_estimate=cost(3),
        name="rotate_tail",
    )(queries, rotation)

    masks = tuple(range(0, shards, 4))
    order = masks + tuple(m ^ 2 for m in masks)
    other = tuple(m ^ 1 for m in order)
    flat = vectors.reshape(page_count * page_rows, full_width)

    def stack(parts, waits, name):
        return pl.pallas_call(
            stack_kernel,
            in_specs=[whole(VMEM)] * len(parts) + [whole(ANY)] * len(waits),
            out_specs=whole(VMEM),
            out_shape=jax.ShapeDtypeStruct((len(parts), *parts[0].shape), BF16),
            compiler_params=params(10 * MIB),
            cost_estimate=cost(1),
            name=name,
        )(*parts, *waits)

    def relay(x, *waits):
        return pl.pallas_call(
            relay_kernel,
            in_specs=[whole(VMEM)] + [whole(ANY)] * len(waits),
            out_specs=whole(VMEM),
            out_shape=jax.ShapeDtypeStruct(x.shape, x.dtype),
            compiler_params=params(4 * MIB),
            cost_estimate=cost(1),
            name="relay",
        )(x, *waits)

    def coarse_scores(order, pieces, waits, before):
        count = 3 + len(waits)
        return pl.pallas_call(
            functools.partial(coarse_kernel, shards, order, block_rows),
            in_specs=[whole(SMEM), whole(VMEM), whole(VMEM)] + [whole(ANY)] * len(waits) + [whole(VMEM)] * len(before),
            out_specs=[whole(VMEM), whole(ANY)],
            out_shape=[
                jax.ShapeDtypeStruct((shards, capacity, block_rows, page_rows), BF16),
                jax.ShapeDtypeStruct((2, len(order), LANES), I32),
            ],
            scratch_shapes=[
                pltpu.VMEM((2, len(order), LANES), I32),
                pltpu.VMEM((len(order), LANES), I32),
                pltpu.SMEM((len(order), LANES), I32),
                pltpu.SemaphoreType.DMA((2,)),
            ],
            input_output_aliases={count: 0} if before else {},
            compiler_params=params(10 * MIB),
            cost_estimate=cost(COARSE_COST),
            name="coarse_scores",
        )(me, pieces, codes, *waits, *before)

    heads = [exchange(chunk, m, shards) if m else chunk for m in masks]
    heads += [exchange(x, 2, shards) for x in heads]
    sent = relay(tail, heads[1], heads[2])
    tails = [exchange(sent, m, shards) if m else tail for m in masks]
    heads_a = stack(heads, tails[1:], "stack_heads")
    heads_b = exchange(heads_a, 1, shards)
    tails += [exchange(x, 2, shards) for x in tails]
    scored, list_a = coarse_scores(order, heads_a, [], [])
    scored, list_b = coarse_scores(other, heads_b, [], [scored])
    returned = lax.all_to_all(scored, "idx", split_axis=0, concat_axis=0, tiled=True)

    found = pl.pallas_call(
        gather_kernel,
        in_specs=[whole(ANY)] * 3,
        out_specs=whole(VMEM),
        out_shape=jax.ShapeDtypeStruct((2, len(order), row_capacity, full_width), BF16),
        scratch_shapes=[
            pltpu.SMEM((shards, LANES), I32),
            pltpu.VMEM(flat.shape, F32),
            pltpu.SemaphoreType.DMA((6,)),
        ],
        compiler_params=params(34 * MIB),
        cost_estimate=cost(GATHER_COST),
        name="gather_rows",
    )(list_a, list_b, flat)
    tails_a = stack(tails, [found], "stack_tails")
    tails_b = exchange(tails_a, 1, shards)

    def scores(part, order, list_ref, heads, tails, before):
        return pl.pallas_call(
            functools.partial(rerank_kernel, part, order),
            in_specs=[whole(ANY)] + [whole(VMEM)] * (3 + len(before)),
            out_specs=whole(VMEM),
            out_shape=jax.ShapeDtypeStruct((shards // 4, 4, row_capacity), F32),
            scratch_shapes=[pltpu.VMEM((len(order), LANES), I32), pltpu.SemaphoreType.DMA],
            compiler_params=params(10 * MIB),
            cost_estimate=cost(RERANK_COST),
            name="rerank_scores",
        )(list_ref, found, heads, tails, *before)

    answers = scores(0, order, list_a, heads_a, tails_a, [])
    answers = scores(1, other, list_b, heads_b, tails_b, [answers])
    own = jnp.stack([exchange(answers[a], 4 * a, shards) if a else answers[a] for a in range(shards // 4)])
    across = exchange(own, 2, shards)
    coarse, placed = pl.pallas_call(
        place_kernel,
        in_specs=[whole(SMEM), whole(VMEM)],
        out_specs=[whole(VMEM)] * 2,
        out_shape=[
            jax.ShapeDtypeStruct((query_rows, probe_count * page_rows), BF16),
            jax.ShapeDtypeStruct((8, LANES), F32),
        ],
        compiler_params=params(10 * MIB),
        cost_estimate=cost(1),
        name="place_scores",
    )(probe_place, returned.reshape(shards * capacity, block_rows, page_rows))
    rerank = pl.pallas_call(
        functools.partial(pick_kernel, shards),
        in_specs=[whole(SMEM)] + [whole(VMEM)] * 6,
        out_specs=whole(VMEM),
        out_shape=jax.ShapeDtypeStruct((cand_count, query_rows), F32),
        scratch_shapes=[pltpu.VMEM((shards, row_capacity), F32)],
        compiler_params=params(10 * MIB),
        cost_estimate=cost(1),
        name="pick_answers",
    )(me, own, across, exchange(own, 1, shards), exchange(own, 3, shards), cand_place, placed).T
    return coarse, rerank


def solution(mesh):
    split = P(("grp", "idx"))
    in_specs = (split, P(), split, split, split, split, split)
    return jax.shard_map(body, mesh=mesh, in_specs=in_specs, out_specs=(split, split), check_vma=False)
```
